256 devices in a mesh: leaf: 64 (over z, y, core), rows: 4 (over x).
Axes of the slice: x: 4, y: 4, z: 8, core: 2. Of those that a mesh axis runs over, the one named last changes fastest.
Arguments:
- samples: bfloat16 [2097152, 256], P(('leaf', 'rows')), may hold values from -40 to 40
- row_order: int32 [16384, 128], P(('leaf', 'rows')), may hold values from 0 to 127, each once within a row
- cluster_map: int32 [16384], P(('leaf', 'rows')), may hold values from 0 to 63, as said below
- leaf_sketch: bfloat16 [256, 128], replicated, may hold values from -0.375 to 0.375
- level_sketch: float32 [3, 256, 128], replicated, may hold values from -0.375 to 0.375
Outputs:
- bases: bfloat16 [4194304, 128], P(('leaf', 'rows'))
- transfers: float32 [64, 3, 128, 128], P('leaf')
- summaries: float32 [64, 128, 256], P('leaf')
The draws below stay inside these ranges and needn't reach their ends.
Inputs may be any that keep to these rules, and one draw needn't show every extreme that they name: `cluster_map`: the 64 blocks of one device name each cluster at most 2 times; in every draw one cluster is named exactly 2 times on every device.
All inputs are finite; a program needn't handle non-finite values.
Results may differ from the reference program's by a relative error of at most 0.023.
Values may be sent and summed in bfloat16 or wider, within the bound.
No kernel may reach another device: no remote copies, remote signals or barrier semaphores. Data moves between devices by JAX's collectives and lax.ppermute only.
A program may use at most 128 MiB of HBM per device.

```python
import math
import jax
import jax.numpy as jnp
from jax import lax

SUB_DEV = 64
BLK = 128
PCOLS = 256
RANK = 128
LEVELS = 3
CLUSTERS = 64
CAPS = 2
BLOCKS = 16384
N_LEAF = 64
N_ROWS = 4


def draw_samples(key, part):
    first, second, third = jax.random.split(jax.random.fold_in(key, 11), 3)
    total_rows = BLOCKS * BLK
    base = jnp.clip(jax.random.normal(first, (total_rows, PCOLS), jnp.float32), -6.0, 6.0)
    mixed = base + 0.6 * jnp.roll(base, 1, axis=1)
    col_scale = jnp.exp(jax.random.uniform(second, (1, PCOLS), jnp.float32, 0.0, math.log(4.0)))
    row_scale = jnp.exp(jax.random.uniform(third, (total_rows, 1), jnp.float32, math.log(0.5), math.log(2.0)))
    return jnp.clip(mixed * col_scale * row_scale, -40.0, 40.0).astype(jnp.bfloat16)


def draw_cluster_map(key, part):
    base_key = jax.random.fold_in(key, 5)
    hottest = jax.random.randint(jax.random.fold_in(base_key, 1), (), 0, CLUSTERS)
    device_count = BLOCKS // SUB_DEV
    device_keys = jax.random.split(jax.random.fold_in(base_key, 2), device_count)

    def one_device(device_key):
        pick_key, order_key = jax.random.split(device_key)
        others = jax.random.permutation(pick_key, (CLUSTERS - 1) * CAPS)[:SUB_DEV - CAPS]
        relative = jnp.concatenate([jnp.zeros((CAPS,), jnp.int32), 1 + others.astype(jnp.int32) // CAPS])
        chosen = (relative + hottest) % CLUSTERS
        return jax.random.permutation(order_key, chosen)
    return jax.vmap(one_device)(device_keys).reshape(BLOCKS).astype(jnp.int32)


def scatter_about(stream_key, extent, deviation, most, kind=jnp.bfloat16):
    result = jax.random.normal(stream_key, extent, jnp.float32) * deviation
    return jnp.minimum(jnp.maximum(result, -most), most).astype(kind)


def setup_inputs(seed: int = 0) -> dict:
    seeds = jax.random.split(jax.random.key(seed), 6)
    samples = draw_samples(jax.random.fold_in(seeds[5], 71), 0)
    row_order = jax.vmap(lambda own: jax.random.permutation(own, BLK))(jax.random.split(seeds[1], BLOCKS)).reshape((BLOCKS, BLK)).astype(jnp.int32)
    cluster_map = draw_cluster_map(jax.random.fold_in(seeds[5], 71), 0)
    leaf_sketch = scatter_about(seeds[3], (PCOLS, RANK), PCOLS ** -0.5, 0.375)
    level_sketch = scatter_about(seeds[4], (LEVELS, PCOLS, RANK), PCOLS ** -0.5, 0.375, jnp.float32)
    return dict(samples=samples, row_order=row_order, cluster_map=cluster_map, leaf_sketch=leaf_sketch, level_sketch=level_sketch)


SHIFT = 0.01

def merge_pair(stacked, sketch_level):
    rows_total = stacked.shape[0]
    rank_cols = sketch_level.shape[1]
    sample_cols = stacked.shape[1]
    projected = jnp.dot(stacked, sketch_level, precision=lax.Precision.HIGHEST)
    gram = jnp.dot(projected.T, projected, precision=lax.Precision.HIGHEST) / rows_total + SHIFT * jnp.eye(rank_cols, dtype=jnp.float32)
    lower_factor = jnp.linalg.cholesky(gram)
    inverse_lower = lax.linalg.triangular_solve(lower_factor, jnp.eye(rank_cols, dtype=jnp.float32), left_side=True, lower=True)
    transfer = jnp.dot(projected, inverse_lower.T, precision=lax.Precision.HIGHEST)
    product = jnp.dot(projected.T, stacked, precision=lax.Precision.HIGHEST)
    parent = jnp.dot(inverse_lower, product, precision=lax.Precision.HIGHEST) * (math.sqrt(sample_cols) / rows_total)
    return (transfer, parent)

def split_apply(sketched, inverse_lower):
    whole = inverse_lower.T
    upper_part = whole.astype(jnp.bfloat16)
    lower_part = (whole - upper_part.astype(jnp.float32)).astype(jnp.bfloat16)
    first = jnp.dot(sketched.astype(jnp.float32), upper_part.astype(jnp.float32), preferred_element_type=jnp.float32)
    second = jnp.dot(sketched.astype(jnp.float32), lower_part.astype(jnp.float32), preferred_element_type=jnp.float32)
    return (first + second).astype(jnp.bfloat16)

def reference(samples, row_order, cluster_map, leaf_sketch, level_sketch):
    devices = N_LEAF * N_ROWS
    blocks = samples.reshape(BLOCKS, BLK, PCOLS)
    ordered = jnp.take_along_axis(blocks, row_order[:, :, None], axis=1)
    maps = cluster_map.reshape(devices, SUB_DEV)
    hits = (maps[:, :, None] == jnp.arange(CLUSTERS, dtype=jnp.int32)[None, None, :]).astype(jnp.int32)
    before = jnp.cumsum(hits, axis=1) - hits
    slot_rank = lax.optimization_barrier(jnp.sum(before * hits, axis=2)).reshape(BLOCKS).astype(jnp.int32)
    device_index = (jnp.arange(BLOCKS, dtype=jnp.int32) // SUB_DEV).astype(jnp.int32)
    source_leaf = device_index // N_ROWS
    source_row = device_index % N_ROWS
    target_device = (cluster_map * N_ROWS + source_row).astype(jnp.int32)
    target_block = (source_leaf * CAPS + slot_rank).astype(jnp.int32)
    buffer = jnp.zeros((devices, CLUSTERS * CAPS, BLK, PCOLS), jnp.bfloat16)
    buffer = buffer.at[target_device, target_block].set(ordered)
    cluster_rows = buffer.reshape(CLUSTERS, N_ROWS * CLUSTERS * CAPS * BLK, PCOLS)
    row_norm = float(N_ROWS * SUB_DEV * BLK)

    def leaf_work(received):
        sketched = jnp.dot(received.astype(jnp.float32), leaf_sketch.astype(jnp.float32), preferred_element_type=jnp.float32).astype(jnp.bfloat16)
        gram = jnp.dot(sketched.T.astype(jnp.float32), sketched.astype(jnp.float32), preferred_element_type=jnp.float32)
        cross = jnp.dot(sketched.T.astype(jnp.float32), received.astype(jnp.float32), preferred_element_type=jnp.float32)
        gram = gram / row_norm + SHIFT * jnp.eye(RANK, dtype=jnp.float32)
        lower_factor = jnp.linalg.cholesky(gram)
        inverse_lower = lax.linalg.triangular_solve(lower_factor, jnp.eye(RANK, dtype=jnp.float32), left_side=True, lower=True)
        basis = split_apply(sketched, inverse_lower)
        summary = jnp.dot(inverse_lower, cross, precision=lax.Precision.HIGHEST) * (math.sqrt(PCOLS) / row_norm)
        return (basis, summary)
    bases, nodes_now = lax.map(leaf_work, cluster_rows)
    cluster_index = jnp.arange(CLUSTERS, dtype=jnp.int32)
    halves = []
    for depth_index in range(LEVELS):
        paired = nodes_now.reshape(-1, 2 * RANK, PCOLS)
        transfer_all, parent_all = jax.vmap(merge_pair, in_axes=(0, None))(paired, level_sketch[depth_index])
        split_all = transfer_all.reshape(-1, 2, RANK, RANK)
        halves.append(split_all[cluster_index >> depth_index + 1, cluster_index >> depth_index & 1])
        nodes_now = parent_all
    summaries = nodes_now[cluster_index >> LEVELS]
    return (bases.reshape(-1, RANK), jnp.stack(halves, axis=1), summaries)
```

```python
import functools
import math

import jax
import jax.numpy as jnp
from jax import lax
from jax.experimental import pallas as pl
from jax.experimental.pallas import tpu as pltpu
from jax.sharding import Mesh, PartitionSpec as P

LEVELS = 3
SHIFT = 0.01
PANEL = 16
HIGHEST = lax.Precision.HIGHEST
F32 = jnp.float32
BF16 = jnp.bfloat16
VMEM_LIMIT = 56 * 2**20

NT = (((1,), (1,)), ((), ()))
TN = (((0,), (0,)), ((), ()))


def exact(a, b, dims=(((1,), (0,)), ((), ()))):
    return lax.dot_general(a, b, dims, precision=HIGHEST, preferred_element_type=F32)


def cholesky_inverse(work, inverse):
    n = inverse.shape[0]
    row = lax.broadcasted_iota(jnp.int32, (PANEL, n), 0)
    for first in range(0, n, PANEL):
        left = work[first : first + PANEL, :n]
        right = work[first : first + PANEL, n:]
        cols = [
            jnp.broadcast_to(left[:, first + j : first + j + 1], (PANEL, n)) for j in range(PANEL)
        ]
        scale = jnp.zeros((PANEL, n), F32)
        for j in range(PANEL):
            pivot = cols[j][j : j + 1]
            factor = jnp.where(row > j, cols[j] * (1.0 / pivot), 0.0)
            scale = jnp.where(row == j, lax.rsqrt(pivot), scale)
            left = left - factor * left[j : j + 1]
            right = right - factor * right[j : j + 1]
            for k in range(j + 1, PANEL):
                cols[k] = cols[k] - factor * cols[k][j : j + 1]
        left = left * scale
        right = right * scale
        inverse[first : first + PANEL, :] = right
        rest = first + PANEL
        if rest < n:
            both = jnp.concatenate([left, right], axis=1)
            update = exact(left, both, TN)
            work[rest:, :] = work[rest:, :] - update[rest:, :]


def identity(n):
    shape = (n, n)
    return (
        lax.broadcasted_iota(jnp.int32, shape, 0) == lax.broadcasted_iota(jnp.int32, shape, 1)
    ).astype(F32)


def prep_kernel(
    map_ref, place_ref, order_ref, samples_ref, sketch_ref,
    packed_ref, send_a, send_b, keep_a, keep_b,
    parts, ordered, slots, count, columns,
):
    blocks, rows, width = samples_ref.shape
    zs, ys, cores, xs = 8, 4, 2, 4
    rank = sketch_ref.shape[1]
    group = columns.shape[0]
    each = blocks // group
    step = pl.program_id(0)

    @pl.when(step == 0)
    def _():
        clusters = count.shape[0]

        def clear(c, _):
            count[c] = 0
            slots[2 * c] = blocks
            slots[2 * c + 1] = blocks
            return 0

        lax.fori_loop(0, clusters, clear, 0)

        def place(b, _):
            c = map_ref[b]
            slots[2 * c + count[c]] = b
            count[c] = count[c] + 1
            return 0

        lax.fori_loop(0, blocks, place, 0)
        parts[blocks] = jnp.zeros((2 * rank, rows), BF16)
        ordered[blocks] = jnp.zeros((rows, rank), BF16)
        turned = order_ref[...].astype(F32).T
        for g in range(group):
            columns[g] = turned[:, g * each : (g + 1) * each]
        sketch_t = sketch_ref[...].astype(F32).T.astype(BF16)
        lane = lax.broadcasted_iota(jnp.int32, (rows, rows), 1).astype(F32)

        def some(g, _):
            column = columns[g]
            for u in range(each):
                b = g * each + u
                value = lax.dot_general(
                    sketch_t, samples_ref[b], NT, preferred_element_type=F32
                )
                high = value.astype(BF16)
                low = (value - high.astype(F32)).astype(BF16)
                parts[b, :rank, :] = high
                parts[b, rank:, :] = low
                pick = (jnp.broadcast_to(column[:, u : u + 1], (rows, rows)) == lane).astype(F32)
                ordered[b] = lax.dot_general(
                    pick.astype(BF16), high, NT, preferred_element_type=F32
                ).astype(BF16)
            return 0

        lax.fori_loop(0, group, some, 0)

    my_z, my_y, my_core, my_x = (place_ref[i] for i in range(4))
    y = lax.rem(my_y + step, ys)
    quarter = rows // 2 // xs

    def one(z_rel, _):
        z = lax.rem(my_z + z_rel, zs)
        for k_rel, out_a, out_b in ((0, keep_a, keep_b), (1, send_a, send_b)):
            core = my_core if k_rel == 0 else 1 - my_core
            cluster = (z * ys + y) * cores + core
            b0 = slots[2 * cluster]
            b1 = slots[2 * cluster + 1]
            packed_ref[z, 0, core, :rows, :] = ordered[b0]
            packed_ref[z, 0, core, rows:, :] = ordered[b1]
            lhs = jnp.concatenate([parts[b0], parts[b1]], axis=1)
            rhs = jnp.concatenate(
                [samples_ref[jnp.minimum(b0, blocks - 1)], samples_ref[jnp.minimum(b1, blocks - 1)]],
                axis=0,
            )
            both = jnp.dot(lhs, rhs, preferred_element_type=F32)
            total = both[:rank] + both[rank:]
            for x in range(xs):
                x_rel = lax.rem(x - my_x + xs, xs)
                out_a[0, z_rel, x_rel] = total[x * quarter : (x + 1) * quarter]
                out_b[0, z_rel, x_rel] = total[rank // 2 + x * quarter : rank // 2 + (x + 1) * quarter]
        return 0

    lax.fori_loop(0, zs, one, 0, unroll=2)


def prepare(samples, row_order, cluster_map, leaf_sketch, place):
    blocks, rows = row_order.shape
    width = samples.shape[1]
    rank = leaf_sketch.shape[1]
    samples = samples.reshape(blocks, rows, width)
    zs, ys, cores, xs = 8, 4, 2, 4
    quarter = rows // 2 // xs
    chunk = jax.ShapeDtypeStruct((ys, zs, xs, quarter, width), F32)
    chunk_spec = pl.BlockSpec((1, zs, xs, quarter, width), lambda i, m, p: (i, 0, 0, 0, 0))
    packed = jax.ShapeDtypeStruct((zs, ys, cores, 2 * rows, rank), BF16)
    return pl.pallas_call(
        prep_kernel,
        out_shape=(packed, chunk, chunk, chunk, chunk),
        grid_spec=pltpu.PrefetchScalarGridSpec(
            num_scalar_prefetch=2,
            grid=(ys,),
            in_specs=[
                pl.BlockSpec(row_order.shape, lambda i, m, p: (0, 0)),
                pl.BlockSpec(samples.shape, lambda i, m, p: (0, 0, 0)),
                pl.BlockSpec(leaf_sketch.shape, lambda i, m, p: (0, 0)),
            ],
            out_specs=[
                pl.BlockSpec(
                    (zs, 1, cores, 2 * rows, rank),
                    lambda i, m, p: (0, lax.rem(p[1] + i, 4), 0, 0, 0),
                )
            ]
            + [chunk_spec] * 4,
            scratch_shapes=[
                pltpu.VMEM((blocks + 1, 2 * rank, rows), BF16),
                pltpu.VMEM((blocks + 1, rows, rank), BF16),
                pltpu.SMEM((2 * zs * ys * cores,), jnp.int32),
                pltpu.SMEM((zs * ys * cores,), jnp.int32),
                pltpu.VMEM((8, rows, blocks // 8), F32),
            ],
        ),
        compiler_params=pltpu.CompilerParams(vmem_limit_bytes=VMEM_LIMIT),
        cost_estimate=pl.CostEstimate(
            flops=6 * 10**9, bytes_accessed=16 * 2**20, transcendentals=0
        ),
        name="prepare",
    )(cluster_map, place, row_order, samples, leaf_sketch)


def leaf_kernel(row_norm, place_ref, c0, c1, c2, c3, sketch_ref, parts_ref, node_ref, cross, work, inverse):
    rank, width = node_ref.shape
    quarter = rank // 8
    my_x = place_ref[3]
    for rel, chunk in enumerate((c0, c1, c2, c3)):
        start = pl.multiple_of(lax.rem(my_x + rel, 4) * quarter, quarter)
        cross[pl.ds(start, quarter), :] = chunk[:quarter, :]
        cross[pl.ds(start + rank // 2, quarter), :] = chunk[quarter:, :]
    eye = identity(rank)
    gram = exact(cross[...], sketch_ref[...].astype(F32)) / row_norm + SHIFT * eye
    work[:, :rank] = gram
    work[:, rank:] = eye
    cholesky_inverse(work, inverse)
    whole = inverse[...]
    high = whole.astype(BF16)
    parts_ref[:, :rank] = high
    parts_ref[:, rank:] = (whole - high.astype(F32)).astype(BF16)
    node_ref[...] = exact(whole, cross[...]) * (math.sqrt(width) / row_norm)


def leaf_node(place, chunks, leaf_sketch, row_norm):
    rank = leaf_sketch.shape[1]
    width = leaf_sketch.shape[0]
    vmem = pl.BlockSpec(memory_space=pltpu.VMEM)
    return pl.pallas_call(
        functools.partial(leaf_kernel, row_norm),
        out_shape=(
            jax.ShapeDtypeStruct((rank, 2 * rank), BF16),
            jax.ShapeDtypeStruct((rank, width), F32),
        ),
        in_specs=[pl.BlockSpec(memory_space=pltpu.SMEM)] + [vmem] * 5,
        out_specs=(vmem, vmem),
        scratch_shapes=[
            pltpu.VMEM((rank, width), F32),
            pltpu.VMEM((rank, 2 * rank), F32),
            pltpu.VMEM((rank, rank), F32),
        ],
        compiler_params=pltpu.CompilerParams(vmem_limit_bytes=16 * 2**20),
        cost_estimate=pl.CostEstimate(flops=10**10, bytes_accessed=2**20, transcendentals=0),
        name="leaf_node",
    )(place, *chunks, leaf_sketch)


def merge_kernel(own_ref, other_ref, sketch_ref, transfer_ref, node_ref, work, inverse):
    rank, width = node_ref.shape
    total = 2.0 * rank
    sketch = sketch_ref[...]
    own, other = own_ref[...], other_ref[...]
    own_z = exact(own, sketch)
    other_z = exact(other, sketch)
    z = jnp.concatenate([own_z, other_z], axis=0)
    stacked = jnp.concatenate([own, other], axis=0)
    z_t = z.T
    gram = exact(z_t, z) / total
    product = exact(z_t, stacked)
    eye = identity(rank)
    work[:, :rank] = gram + SHIFT * eye
    work[:, rank:] = eye
    cholesky_inverse(work, inverse)
    whole = inverse[...]
    node_ref[...] = exact(whole, product) * (math.sqrt(width) / total)
    transfer_ref[...] = exact(own_z, whole, NT)


def merge(own, other, sketch):
    rank, width = own.shape
    vmem = pl.BlockSpec(memory_space=pltpu.VMEM)
    return pl.pallas_call(
        merge_kernel,
        out_shape=(
            jax.ShapeDtypeStruct((rank, rank), F32),
            jax.ShapeDtypeStruct((rank, width), F32),
        ),
        in_specs=[vmem] * 3,
        out_specs=(vmem, vmem),
        scratch_shapes=[pltpu.VMEM((rank, 2 * rank), F32), pltpu.VMEM((rank, rank), F32)],
        compiler_params=pltpu.CompilerParams(vmem_limit_bytes=16 * 2**20),
        cost_estimate=pl.CostEstimate(flops=10**10, bytes_accessed=2**20, transcendentals=0),
        name="merge",
    )(own, other, sketch)


def bases_kernel(rows_ref, parts_ref, out_ref):
    rows = rows_ref[...]
    out_ref[...] = lax.dot_general(
        jnp.concatenate([rows, rows], axis=1), parts_ref[...], NT, preferred_element_type=F32
    ).astype(BF16)


def bases(rows, parts):
    total, rank = rows.shape
    tile = 2048
    return pl.pallas_call(
        bases_kernel,
        out_shape=jax.ShapeDtypeStruct((total, rank), BF16),
        grid=(total // tile,),
        in_specs=[
            pl.BlockSpec((tile, rank), lambda i: (i, 0)),
            pl.BlockSpec(parts.shape, lambda i: (0, 0)),
        ],
        out_specs=pl.BlockSpec((tile, rank), lambda i: (i, 0)),
        compiler_params=pltpu.CompilerParams(vmem_limit_bytes=32 * 2**20),
        cost_estimate=pl.CostEstimate(
            flops=4 * total * rank * rank, bytes_accessed=4 * total * rank, transcendentals=0
        ),
        name="bases",
    )(rows, parts)


def shift(value, axis, distance):
    size = lax.axis_size(axis)
    return lax.ppermute(value, axis, [(i, (i + distance) % size) for i in range(size)])


def scatter_ring(chunks, axis):
    half = chunks[0].shape[0] // 2
    low = [c[:half] for c in chunks]
    high = [c[half:] for c in chunks]
    up_far = shift(low[2], axis, 1)
    down_far = shift(high[2], axis, -1)
    up_near = shift(high[1], axis, 1)
    down_near = shift(low[3], axis, -1)
    up = shift(low[1] + up_far, axis, 1)
    down = shift(high[3] + down_far, axis, -1)
    return jnp.concatenate([low[0] + down_near + up, high[0] + up_near + down], axis=0)


def body(samples, row_order, cluster_map, leaf_sketch, level_sketch):
    place = jnp.stack([lax.axis_index(a) for a in ("z", "y", "core", "x")]).astype(jnp.int32)
    rows = row_order.shape[1]
    rank = leaf_sketch.shape[1]
    leaf = ("z", "y", "core")
    row_norm = float(lax.axis_size("x") * samples.shape[0])
    packed, send_a, send_b, keep_a, keep_b = prepare(
        samples, row_order, cluster_map, leaf_sketch, place
    )
    clusters = lax.axis_size(leaf)
    received = lax.all_to_all(
        packed.reshape(clusters, 2 * rows, rank), leaf, split_axis=0, concat_axis=0, tiled=True
    ).reshape(-1, rank)
    part_a = keep_a + shift(send_a, "core", 1)
    part_b = keep_b + shift(send_b, "core", 1)
    part_a = scatter_ring([part_a[:, :, r] for r in range(4)], "x")
    part_b = scatter_ring([part_b[r] for r in range(4)], "y")
    part_a = scatter_ring([part_a[r] for r in range(4)], "y")
    part_b = scatter_ring([part_b[:, r] for r in range(4)], "x")
    part = jnp.concatenate([part_a, part_b], axis=1)
    total = part[0]
    for r in range(1, 8):
        total = total + shift(part[r], "z", r)
    chunks = [total] + [shift(total, "x", -r) for r in range(1, 4)]
    parts, node = leaf_node(place, chunks, leaf_sketch, row_norm)
    halves = []
    for depth, (axis, bit) in enumerate((("core", 1), ("y", 1), ("y", 2))):
        pairs = [(i, i ^ bit) for i in range(lax.axis_size(axis))]
        other = lax.ppermute(node, axis, pairs)
        half, node = merge(node, other, level_sketch[depth])
        halves.append(half)
    basis = bases(received, parts)
    return (basis, jnp.stack(halves, axis=0)[None], node[None])


def solution(mesh):
    grid = Mesh(mesh.devices.reshape(8, 4, 2, 4), ("z", "y", "core", "x"))
    every = ("z", "y", "core", "x")
    leaf = ("z", "y", "core")
    in_specs = (P(every, None), P(every, None), P(every), P(), P())
    out_specs = (P(every, None), P(leaf, None, None, None), P(leaf, None, None))
    return jax.shard_map(body, mesh=grid, in_specs=in_specs, out_specs=out_specs, check_vma=False)
```

```python
import functools
import math

import jax
import jax.numpy as jnp
from jax import lax
from jax.experimental import pallas as pl
from jax.experimental.pallas import tpu as pltpu
from jax.sharding import Mesh, PartitionSpec as P

LEVELS = 3
SHIFT = 0.01
PANEL = 16
HIGHEST = lax.Precision.HIGHEST
F32 = jnp.float32
BF16 = jnp.bfloat16
VMEM_LIMIT = 56 * 2**20

NT = (((1,), (1,)), ((), ()))
TN = (((0,), (0,)), ((), ()))


def exact(a, b, dims=(((1,), (0,)), ((), ()))):
    return lax.dot_general(a, b, dims, precision=HIGHEST, preferred_element_type=F32)


def cholesky_inverse(work, inverse):
    n = inverse.shape[0]
    row = lax.broadcasted_iota(jnp.int32, (PANEL, n), 0)
    for first in range(0, n, PANEL):
        left = work[first : first + PANEL, :n]
        right = work[first : first + PANEL, n:]
        cols = [
            jnp.broadcast_to(left[:, first + j : first + j + 1], (PANEL, n)) for j in range(PANEL)
        ]
        scale = jnp.zeros((PANEL, n), F32)
        for j in range(PANEL):
            pivot = cols[j][j : j + 1]
            factor = jnp.where(row > j, cols[j] * (1.0 / pivot), 0.0)
            scale = jnp.where(row == j, lax.rsqrt(pivot), scale)
            left = left - factor * left[j : j + 1]
            right = right - factor * right[j : j + 1]
            for k in range(j + 1, PANEL):
                cols[k] = cols[k] - factor * cols[k][j : j + 1]
        left = left * scale
        right = right * scale
        inverse[first : first + PANEL, :] = right
        rest = first + PANEL
        if rest < n:
            both = jnp.concatenate([left, right], axis=1)
            update = exact(left, both, TN)
            work[rest:, :] = work[rest:, :] - update[rest:, :]


def identity(n):
    shape = (n, n)
    return (
        lax.broadcasted_iota(jnp.int32, shape, 0) == lax.broadcasted_iota(jnp.int32, shape, 1)
    ).astype(F32)


def prep_kernel(
    map_ref, place_ref, order_ref, samples_hbm, sketch_ref,
    first_ref, second_ref, send_a, send_b, keep_a, keep_b,
    parts, ordered, slots, count, columns, samples_ref, arrived,
):
    blocks, rows, width = samples_ref.shape
    zs, ys, cores, xs = 8, 4, 2, 4
    rank = sketch_ref.shape[1]
    group = columns.shape[0]
    each = blocks // group
    step = pl.program_id(0)

    def load(g):
        some = pl.ds(g * each, each)
        return pltpu.make_async_copy(samples_hbm.at[some], samples_ref.at[some], arrived.at[g])

    @pl.when(step == 0)
    def _():
        for g in range(group):
            load(g).start()
        clusters = count.shape[0]

        def clear(c, _):
            count[c] = 0
            slots[2 * c] = blocks
            slots[2 * c + 1] = blocks
            return 0

        lax.fori_loop(0, clusters, clear, 0)

        def place(b, _):
            c = map_ref[b]
            slots[2 * c + count[c]] = b
            count[c] = count[c] + 1
            return 0

        lax.fori_loop(0, blocks, place, 0)
        parts[blocks] = jnp.zeros((2 * rank, rows), BF16)
        ordered[blocks] = jnp.zeros((rows, rank), BF16)
        turned = order_ref[...].astype(F32).T
        for g in range(group):
            columns[g] = turned[:, g * each : (g + 1) * each]
        sketch_t = sketch_ref[...].astype(F32).T.astype(BF16)
        lane = lax.broadcasted_iota(jnp.int32, (rows, rows), 1).astype(F32)

        def some(g, _):
            load(g).wait()
            column = columns[g]
            for u in range(each):
                b = g * each + u
                value = lax.dot_general(
                    sketch_t, samples_ref[b], NT, preferred_element_type=F32
                )
                high = value.astype(BF16)
                low = (value - high.astype(F32)).astype(BF16)
                parts[b, :rank, :] = high
                parts[b, rank:, :] = low
                pick = (jnp.broadcast_to(column[:, u : u + 1], (rows, rows)) == lane).astype(F32)
                ordered[b] = lax.dot_general(
                    pick.astype(BF16), high, NT, preferred_element_type=F32
                ).astype(BF16)
            return 0

        lax.fori_loop(0, group, some, 0)

    my_z, my_y, my_core, my_x = (place_ref[i] for i in range(4))
    y = lax.rem(my_y + step, ys)
    quarter = rows // 2 // xs

    def one(z_rel, _):
        flip = ((z_rel & 1) << 2) | (z_rel & 2) | (z_rel >> 2)
        z = my_z ^ flip
        for k_rel, out_a, out_b in ((0, keep_a, keep_b), (1, send_a, send_b)):
            core = my_core if k_rel == 0 else 1 - my_core
            cluster = (z * ys + y) * cores + core
            b0 = slots[2 * cluster]
            b1 = slots[2 * cluster + 1]
            out = first_ref if k_rel == 0 else second_ref
            out[z, 0, :rows] = ordered[b0]
            out[z, 0, rows:] = ordered[b1]
            lhs = jnp.concatenate([parts[b0], parts[b1]], axis=1)
            rhs = jnp.concatenate(
                [samples_ref[jnp.minimum(b0, blocks - 1)], samples_ref[jnp.minimum(b1, blocks - 1)]],
                axis=0,
            )
            both = jnp.dot(lhs, rhs, preferred_element_type=F32)
            total = both[:rank] + both[rank:]
            for x in range(xs):
                x_rel = lax.rem(x - my_x + xs, xs)
                out_a[x_rel, 0, 0, z_rel] = total[x * quarter : (x + 1) * quarter]
                out_b[0, x_rel, z_rel] = total[rank // 2 + x * quarter : rank // 2 + (x + 1) * quarter]
        return 0

    lax.fori_loop(0, zs, one, 0, unroll=8)


def prepare(samples, row_order, cluster_map, leaf_sketch, place):
    blocks, rows = row_order.shape
    width = samples.shape[1]
    rank = leaf_sketch.shape[1]
    samples = samples.reshape(blocks, rows, width)
    zs, ys, cores, xs = 8, 4, 2, 4
    quarter = rows // 2 // xs
    chunk_a = jax.ShapeDtypeStruct((xs, 2, ys // 2, zs, quarter, width), F32)
    chunk_b = jax.ShapeDtypeStruct((ys, xs, zs, quarter, width), F32)
    spec_a = pl.BlockSpec((xs, 1, 1, zs, quarter, width), lambda i, m, p: (0, i // 2, i % 2, 0, 0, 0))
    spec_b = pl.BlockSpec((1, xs, zs, quarter, width), lambda i, m, p: (i, 0, 0, 0, 0))
    packed = jax.ShapeDtypeStruct((zs, ys, 2 * rows, rank), BF16)
    packed_spec = pl.BlockSpec(
        (zs, 1, 2 * rows, rank), lambda i, m, p: (0, lax.rem(p[1] + i, 4), 0, 0)
    )
    return pl.pallas_call(
        prep_kernel,
        out_shape=(packed, packed, chunk_a, chunk_b, chunk_a, chunk_b),
        grid_spec=pltpu.PrefetchScalarGridSpec(
            num_scalar_prefetch=2,
            grid=(ys,),
            in_specs=[
                pl.BlockSpec(row_order.shape, lambda i, m, p: (0, 0)),
                pl.BlockSpec(memory_space=pl.ANY),
                pl.BlockSpec(leaf_sketch.shape, lambda i, m, p: (0, 0)),
            ],
            out_specs=[packed_spec, packed_spec, spec_a, spec_b, spec_a, spec_b],
            scratch_shapes=[
                pltpu.VMEM((blocks + 1, 2 * rank, rows), BF16),
                pltpu.VMEM((blocks + 1, rows, rank), BF16),
                pltpu.SMEM((2 * zs * ys * cores,), jnp.int32),
                pltpu.SMEM((zs * ys * cores,), jnp.int32),
                pltpu.VMEM((8, rows, blocks // 8), F32),
                pltpu.VMEM(samples.shape, BF16),
                pltpu.SemaphoreType.DMA((8,)),
            ],
        ),
        compiler_params=pltpu.CompilerParams(vmem_limit_bytes=VMEM_LIMIT),
        cost_estimate=pl.CostEstimate(
            flops=6 * 10**9, bytes_accessed=16 * 2**20, transcendentals=0
        ),
        name="prepare",
    )(cluster_map, place, row_order, samples, leaf_sketch)


def leaf_kernel(row_norm, place_ref, c0, c1, c2, sketch_ref, parts_ref, node_ref, cross, work, inverse):
    rank, width = node_ref.shape
    quarter = rank // 8
    my_x = place_ref[3]
    for rel, chunk in enumerate((c0, c1, c2.at[0], c2.at[1])):
        start = pl.multiple_of((my_x ^ rel) * quarter, quarter)
        cross[pl.ds(start, quarter), :] = chunk[:quarter, :]
        cross[pl.ds(start + rank // 2, quarter), :] = chunk[quarter:, :]
    eye = identity(rank)
    gram = exact(cross[...], sketch_ref[...].astype(F32)) / row_norm + SHIFT * eye
    work[:, :rank] = gram
    work[:, rank:] = eye
    cholesky_inverse(work, inverse)
    whole = inverse[...]
    high = whole.astype(BF16)
    parts_ref[:, :rank] = high
    parts_ref[:, rank:] = (whole - high.astype(F32)).astype(BF16)
    node_ref[...] = exact(whole, cross[...]) * (math.sqrt(width) / row_norm)


def leaf_node(place, chunks, leaf_sketch, row_norm):
    rank = leaf_sketch.shape[1]
    width = leaf_sketch.shape[0]
    vmem = pl.BlockSpec(memory_space=pltpu.VMEM)
    return pl.pallas_call(
        functools.partial(leaf_kernel, row_norm),
        out_shape=(
            jax.ShapeDtypeStruct((rank, 2 * rank), BF16),
            jax.ShapeDtypeStruct((rank, width), F32),
        ),
        in_specs=[pl.BlockSpec(memory_space=pltpu.SMEM)] + [vmem] * 4,
        out_specs=(vmem, vmem),
        scratch_shapes=[
            pltpu.VMEM((rank, width), F32),
            pltpu.VMEM((rank, 2 * rank), F32),
            pltpu.VMEM((rank, rank), F32),
        ],
        compiler_params=pltpu.CompilerParams(vmem_limit_bytes=16 * 2**20),
        cost_estimate=pl.CostEstimate(flops=10**10, bytes_accessed=2**20, transcendentals=0),
        name="leaf_node",
    )(place, *chunks, leaf_sketch)


def merge_kernel(own_ref, other_ref, sketch_ref, transfer_ref, node_ref, work, inverse):
    rank, width = node_ref.shape
    total = 2.0 * rank
    sketch = sketch_ref[...]
    own, other = own_ref[...], other_ref[...]
    own_z = exact(own, sketch)
    other_z = exact(other, sketch)
    z = jnp.concatenate([own_z, other_z], axis=0)
    stacked = jnp.concatenate([own, other], axis=0)
    z_t = z.T
    gram = exact(z_t, z) / total
    product = exact(z_t, stacked)
    eye = identity(rank)
    work[:, :rank] = gram + SHIFT * eye
    work[:, rank:] = eye
    cholesky_inverse(work, inverse)
    whole = inverse[...]
    node_ref[...] = exact(whole, product) * (math.sqrt(width) / total)
    transfer_ref[...] = exact(own_z, whole, NT)


def merge(own, other, sketch):
    rank, width = own.shape
    vmem = pl.BlockSpec(memory_space=pltpu.VMEM)
    return pl.pallas_call(
        merge_kernel,
        out_shape=(
            jax.ShapeDtypeStruct((rank, rank), F32),
            jax.ShapeDtypeStruct((rank, width), F32),
        ),
        in_specs=[vmem] * 3,
        out_specs=(vmem, vmem),
        scratch_shapes=[pltpu.VMEM((rank, 2 * rank), F32), pltpu.VMEM((rank, rank), F32)],
        compiler_params=pltpu.CompilerParams(vmem_limit_bytes=16 * 2**20),
        cost_estimate=pl.CostEstimate(flops=10**10, bytes_accessed=2**20, transcendentals=0),
        name="merge",
    )(own, other, sketch)


def bases_kernel(place_ref, rows_ref, parts_ref, *refs):
    out_ref = refs[-1]
    rows = rows_ref[...].reshape(-1, rows_ref.shape[-1])
    out_ref[...] = (
        lax.dot_general(
            jnp.concatenate([rows, rows], axis=1), parts_ref[...], NT, preferred_element_type=F32
        )
        .astype(BF16)
        .reshape(out_ref.shape)
    )


def bases(place, rows, parts, other, before=None):
    sources, height, rank = rows.shape
    tile = 8
    args = (place, rows, parts)
    in_specs = [
        pl.BlockSpec((tile, height, rank), lambda i, p: (i, 0, 0)),
        pl.BlockSpec(parts.shape, lambda i, p: (0, 0)),
    ]
    aliases = {}
    if before is not None:
        args += (before,)
        in_specs.append(pl.BlockSpec(memory_space=pl.ANY))
        aliases = {3: 0}
    total = sources * height
    return pl.pallas_call(
        bases_kernel,
        out_shape=jax.ShapeDtypeStruct((sources, 2, height, rank), BF16),
        grid_spec=pltpu.PrefetchScalarGridSpec(
            num_scalar_prefetch=1,
            grid=(sources // tile,),
            in_specs=in_specs,
            out_specs=pl.BlockSpec(
                (tile, 1, height, rank), lambda i, p: (i, p[2] ^ other, 0, 0)
            ),
        ),
        input_output_aliases=aliases,
        compiler_params=pltpu.CompilerParams(vmem_limit_bytes=32 * 2**20),
        cost_estimate=pl.CostEstimate(
            flops=4 * total * rank * rank, bytes_accessed=4 * total * rank, transcendentals=0
        ),
        name="bases",
    )(*args)


def shift(value, axis, distance):
    size = lax.axis_size(axis)
    return lax.ppermute(value, axis, [(i, (i + distance) % size) for i in range(size)])


def swap(value, axis, mask):
    return lax.ppermute(value, axis, [(i, i ^ mask) for i in range(lax.axis_size(axis))])


def scatter_ring(term, axis):
    up = shift(term(3, 2), axis, 1)
    down = shift(term(5, 2), axis, -1)
    up_last = shift(term(2, 1) + up[1:], axis, 1)
    down_last = shift(term(7, 1) + down[:1], axis, -1)
    own = term(0, 2)
    return own[0] + down[1] + up_last[0], own[1] + up[0] + down_last[0]


def body(samples, row_order, cluster_map, leaf_sketch, level_sketch):
    place = jnp.stack([lax.axis_index(a) for a in ("z", "y", "core", "x")]).astype(jnp.int32)
    rows = row_order.shape[1]
    rank = leaf_sketch.shape[1]
    row_norm = float(lax.axis_size("x") * samples.shape[0])
    first, second, send_a, send_b, keep_a, keep_b = prepare(
        samples, row_order, cluster_map, leaf_sketch, place
    )

    def to_cluster(packed):
        packed = packed.reshape(-1, 2 * rows, rank)
        return lax.all_to_all(packed, ("z", "y"), split_axis=0, concat_axis=0, tiled=True)

    first = to_cluster(first)
    got_a = swap(send_a, "core", 1)
    got_b = swap(send_b, "core", 1)
    second = swap(second, "core", 1)
    keep_a, got_a = (v.reshape(8, 2, 8, -1, v.shape[-1]) for v in (keep_a, got_a))
    keep_b, got_b = (v.reshape(8, 2, 8, -1, v.shape[-1]) for v in (keep_b, got_b))
    low_a, high_a = scatter_ring(lambda i, n: keep_a[i : i + n] + got_a[i : i + n], "x")
    low_b, high_b = scatter_ring(lambda i, n: keep_b[i : i + n] + got_b[i : i + n], "y")
    part_a = jnp.concatenate([low_a, high_a], axis=0).reshape(8, 4, -1, low_a.shape[-1])
    part_b = jnp.concatenate([low_b, high_b], axis=0).reshape(8, 4, -1, low_b.shape[-1])
    low_a, high_a = scatter_ring(lambda i, n: part_a[i : i + n], "y")
    low_b, high_b = scatter_ring(lambda i, n: part_b[i : i + n], "x")
    part_a = jnp.concatenate([low_a, high_a], axis=0)
    part_b = jnp.concatenate([low_b, high_b], axis=0)
    total = jnp.concatenate([part_a, part_b], axis=1)
    for mask in (1, 2, 4):
        half = total.shape[0] // 2
        total = total[:half] + swap(total[half:], "z", mask)
    second, total = lax.optimization_barrier((second, total))
    second = to_cluster(second)
    near = swap(total, "x", 1)
    far = swap(jnp.concatenate([total, near], axis=0), "x", 2)
    parts, node = leaf_node(place, (total[0], near[0], far), leaf_sketch, row_norm)
    halves = []
    for depth, (axis, bit) in enumerate((("core", 1), ("y", 1), ("y", 2))):
        other = swap(node, axis, bit)
        half, node = merge(node, other, level_sketch[depth])
        halves.append(half)
    basis = bases(place, second, parts, 1, bases(place, first, parts, 0)).reshape(-1, rank)
    return (basis, jnp.stack(halves, axis=0)[None], node[None])


def solution(mesh):
    grid = Mesh(mesh.devices.reshape(8, 4, 2, 4), ("z", "y", "core", "x"))
    every = ("z", "y", "core", "x")
    leaf = ("z", "y", "core")
    in_specs = (P(every, None), P(every, None), P(every), P(), P())
    out_specs = (P(every, None), P(leaf, None, None, None), P(leaf, None, None))
    return jax.shard_map(body, mesh=grid, in_specs=in_specs, out_specs=out_specs, check_vma=False)
```

```python
import functools
import math

import jax
import jax.numpy as jnp
from jax import lax
from jax.experimental import pallas as pl
from jax.experimental.pallas import tpu as pltpu
from jax.sharding import Mesh, PartitionSpec as P

LEVELS = 3
SHIFT = 0.01
PANEL = 16
HIGHEST = lax.Precision.HIGHEST
F32 = jnp.float32
BF16 = jnp.bfloat16
VMEM_LIMIT = 56 * 2**20

NT = (((1,), (1,)), ((), ()))
TN = (((0,), (0,)), ((), ()))


def exact(a, b, dims=(((1,), (0,)), ((), ()))):
    return lax.dot_general(a, b, dims, precision=HIGHEST, preferred_element_type=F32)


def cholesky_inverse(work, inverse):
    n = inverse.shape[0]
    row = lax.broadcasted_iota(jnp.int32, (PANEL, n), 0)
    for first in range(0, n, PANEL):
        left = work[first : first + PANEL, :n]
        right = work[first : first + PANEL, n:]
        cols = [
            jnp.broadcast_to(left[:, first + j : first + j + 1], (PANEL, n)) for j in range(PANEL)
        ]
        scale = jnp.zeros((PANEL, n), F32)
        for j in range(PANEL):
            pivot = cols[j][j : j + 1]
            factor = jnp.where(row > j, cols[j] * (1.0 / pivot), 0.0)
            scale = jnp.where(row == j, lax.rsqrt(pivot), scale)
            left = left - factor * left[j : j + 1]
            right = right - factor * right[j : j + 1]
            for k in range(j + 1, PANEL):
                cols[k] = cols[k] - factor * cols[k][j : j + 1]
        left = left * scale
        right = right * scale
        inverse[first : first + PANEL, :] = right
        rest = first + PANEL
        if rest < n:
            both = jnp.concatenate([left, right], axis=1)
            update = exact(left, both, TN)
            work[rest:, :] = work[rest:, :] - update[rest:, :]


def identity(n):
    shape = (n, n)
    return (
        lax.broadcasted_iota(jnp.int32, shape, 0) == lax.broadcasted_iota(jnp.int32, shape, 1)
    ).astype(F32)


def prep_kernel(
    map_ref, place_ref, order_ref, samples_hbm, sketch_ref,
    first_ref, second_ref, send_a, send_b, keep_a, keep_b,
    parts, ordered, slots, count, columns, samples_ref, arrived,
):
    blocks, rows, width = samples_ref.shape
    zs, ys, cores, xs = 8, 4, 2, 4
    rank = sketch_ref.shape[1]
    group = columns.shape[0]
    each = blocks // group
    step = pl.program_id(0)

    def load(g):
        some = pl.ds(g * each, each)
        return pltpu.make_async_copy(samples_hbm.at[some], samples_ref.at[some], arrived.at[g])

    @pl.when(step == 0)
    def _():
        for g in range(group):
            load(g).start()
        clusters = count.shape[0]

        def clear(c, _):
            count[c] = 0
            slots[2 * c] = blocks
            slots[2 * c + 1] = blocks
            return 0

        lax.fori_loop(0, clusters, clear, 0)

        def place(b, _):
            c = map_ref[b]
            slots[2 * c + count[c]] = b
            count[c] = count[c] + 1
            return 0

        lax.fori_loop(0, blocks, place, 0)
        parts[blocks] = jnp.zeros((2 * rank, rows), BF16)
        ordered[blocks] = jnp.zeros((rows, rank), BF16)
        turned = order_ref[...].astype(F32).T
        for g in range(group):
            columns[g] = turned[:, g * each : (g + 1) * each]
        sketch_t = sketch_ref[...].astype(F32).T.astype(BF16)
        lane = lax.broadcasted_iota(jnp.int32, (rows, rows), 1).astype(F32)

        def some(g, _):
            load(g).wait()
            column = columns[g]
            for u in range(each):
                b = g * each + u
                value = lax.dot_general(
                    sketch_t, samples_ref[b], NT, preferred_element_type=F32
                )
                high = value.astype(BF16)
                low = (value - high.astype(F32)).astype(BF16)
                parts[b, :rank, :] = high
                parts[b, rank:, :] = low
                pick = (jnp.broadcast_to(column[:, u : u + 1], (rows, rows)) == lane).astype(F32)
                ordered[b] = lax.dot_general(
                    pick.astype(BF16), high, NT, preferred_element_type=F32
                ).astype(BF16)
            return 0

        lax.fori_loop(0, group, some, 0)

    my_z, my_y, my_core, my_x = (place_ref[i] for i in range(4))
    y = lax.rem(my_y + step, ys)
    quarter = rows // 2 // xs

    def one(z_rel, _):
        flip = ((z_rel & 1) << 2) | (z_rel & 2) | (z_rel >> 2)
        z = my_z ^ flip
        for k_rel, out_a, out_b in ((0, keep_a, keep_b), (1, send_a, send_b)):
            core = my_core if k_rel == 0 else 1 - my_core
            cluster = (z * ys + y) * cores + core
            b0 = slots[2 * cluster]
            b1 = slots[2 * cluster + 1]
            out = first_ref if k_rel == 0 else second_ref
            out[z, 0, :rows] = ordered[b0]
            out[z, 0, rows:] = ordered[b1]
            lhs = jnp.concatenate([parts[b0], parts[b1]], axis=1)
            rhs = jnp.concatenate(
                [samples_ref[jnp.minimum(b0, blocks - 1)], samples_ref[jnp.minimum(b1, blocks - 1)]],
                axis=0,
            )
            both = jnp.dot(lhs, rhs, preferred_element_type=F32)
            total = both[:rank] + both[rank:]
            for x in range(xs):
                x_rel = lax.rem(x - my_x + xs, xs)
                out_a[x_rel, 0, 0, z_rel] = total[x * quarter : (x + 1) * quarter]
                out_b[0, x_rel, z_rel] = total[rank // 2 + x * quarter : rank // 2 + (x + 1) * quarter]
        return 0

    lax.fori_loop(0, zs, one, 0, unroll=8)


def prepare(samples, row_order, cluster_map, leaf_sketch, place):
    blocks, rows = row_order.shape
    width = samples.shape[1]
    rank = leaf_sketch.shape[1]
    samples = samples.reshape(blocks, rows, width)
    zs, ys, cores, xs = 8, 4, 2, 4
    quarter = rows // 2 // xs
    chunk_a = jax.ShapeDtypeStruct((xs, 2, ys // 2, zs, quarter, width), F32)
    chunk_b = jax.ShapeDtypeStruct((ys, xs, zs, quarter, width), F32)
    spec_a = pl.BlockSpec((xs, 1, 1, zs, quarter, width), lambda i, m, p: (0, i // 2, i % 2, 0, 0, 0))
    spec_b = pl.BlockSpec((1, xs, zs, quarter, width), lambda i, m, p: (i, 0, 0, 0, 0))
    packed = jax.ShapeDtypeStruct((zs, ys, 2 * rows, rank), BF16)
    packed_spec = pl.BlockSpec(
        (zs, 1, 2 * rows, rank), lambda i, m, p: (0, lax.rem(p[1] + i, 4), 0, 0)
    )
    return pl.pallas_call(
        prep_kernel,
        out_shape=(packed, packed, chunk_a, chunk_b, chunk_a, chunk_b),
        grid_spec=pltpu.PrefetchScalarGridSpec(
            num_scalar_prefetch=2,
            grid=(ys,),
            in_specs=[
                pl.BlockSpec(row_order.shape, lambda i, m, p: (0, 0)),
                pl.BlockSpec(memory_space=pl.ANY),
                pl.BlockSpec(leaf_sketch.shape, lambda i, m, p: (0, 0)),
            ],
            out_specs=[packed_spec, packed_spec, spec_a, spec_b, spec_a, spec_b],
            scratch_shapes=[
                pltpu.VMEM((blocks + 1, 2 * rank, rows), BF16),
                pltpu.VMEM((blocks + 1, rows, rank), BF16),
                pltpu.SMEM((2 * zs * ys * cores,), jnp.int32),
                pltpu.SMEM((zs * ys * cores,), jnp.int32),
                pltpu.VMEM((8, rows, blocks // 8), F32),
                pltpu.VMEM(samples.shape, BF16),
                pltpu.SemaphoreType.DMA((8,)),
            ],
        ),
        compiler_params=pltpu.CompilerParams(vmem_limit_bytes=VMEM_LIMIT),
        cost_estimate=pl.CostEstimate(
            flops=6 * 10**9, bytes_accessed=16 * 2**20, transcendentals=0
        ),
        name="prepare",
    )(cluster_map, place, row_order, samples, leaf_sketch)


def leaf_kernel(row_norm, place_ref, c0, c1, c2, sketch_ref, parts_ref, node_ref, cross, work, inverse):
    rank, width = node_ref.shape
    quarter = rank // 8
    my_x = place_ref[3]
    for rel, chunk in enumerate((c0, c1, c2.at[0], c2.at[1])):
        start = pl.multiple_of((my_x ^ rel) * quarter, quarter)
        cross[pl.ds(start, quarter), :] = chunk[:quarter, :]
        cross[pl.ds(start + rank // 2, quarter), :] = chunk[quarter:, :]
    eye = identity(rank)
    gram = exact(cross[...], sketch_ref[...].astype(F32)) / row_norm + SHIFT * eye
    work[:, :rank] = gram
    work[:, rank:] = eye
    cholesky_inverse(work, inverse)
    whole = inverse[...]
    high = whole.astype(BF16)
    parts_ref[:, :rank] = high
    parts_ref[:, rank:] = (whole - high.astype(F32)).astype(BF16)
    node_ref[...] = exact(whole, cross[...]) * (math.sqrt(width) / row_norm)


def leaf_node(place, chunks, leaf_sketch, row_norm):
    rank = leaf_sketch.shape[1]
    width = leaf_sketch.shape[0]
    vmem = pl.BlockSpec(memory_space=pltpu.VMEM)
    return pl.pallas_call(
        functools.partial(leaf_kernel, row_norm),
        out_shape=(
            jax.ShapeDtypeStruct((rank, 2 * rank), BF16),
            jax.ShapeDtypeStruct((rank, width), F32),
        ),
        in_specs=[pl.BlockSpec(memory_space=pltpu.SMEM)] + [vmem] * 4,
        out_specs=(vmem, vmem),
        scratch_shapes=[
            pltpu.VMEM((rank, width), F32),
            pltpu.VMEM((rank, 2 * rank), F32),
            pltpu.VMEM((rank, rank), F32),
        ],
        compiler_params=pltpu.CompilerParams(vmem_limit_bytes=16 * 2**20),
        cost_estimate=pl.CostEstimate(flops=10**10, bytes_accessed=2**20, transcendentals=0),
        name="leaf_node",
    )(place, *chunks, leaf_sketch)


def merge_kernel(own_ref, other_ref, sketch_ref, transfer_ref, node_ref, work, inverse):
    rank, width = node_ref.shape
    total = 2.0 * rank
    sketch = sketch_ref[...]
    own, other = own_ref[...], other_ref[...]
    own_z = exact(own, sketch)
    other_z = exact(other, sketch)
    z = jnp.concatenate([own_z, other_z], axis=0)
    stacked = jnp.concatenate([own, other], axis=0)
    z_t = z.T
    gram = exact(z_t, z) / total
    product = exact(z_t, stacked)
    eye = identity(rank)
    work[:, :rank] = gram + SHIFT * eye
    work[:, rank:] = eye
    cholesky_inverse(work, inverse)
    whole = inverse[...]
    node_ref[...] = exact(whole, product) * (math.sqrt(width) / total)
    transfer_ref[...] = exact(own_z, whole, NT)


def merge(own, other, sketch):
    rank, width = own.shape
    vmem = pl.BlockSpec(memory_space=pltpu.VMEM)
    return pl.pallas_call(
        merge_kernel,
        out_shape=(
            jax.ShapeDtypeStruct((rank, rank), F32),
            jax.ShapeDtypeStruct((rank, width), F32),
        ),
        in_specs=[vmem] * 3,
        out_specs=(vmem, vmem),
        scratch_shapes=[pltpu.VMEM((rank, 2 * rank), F32), pltpu.VMEM((rank, rank), F32)],
        compiler_params=pltpu.CompilerParams(vmem_limit_bytes=16 * 2**20),
        cost_estimate=pl.CostEstimate(flops=10**10, bytes_accessed=2**20, transcendentals=0),
        name="merge",
    )(own, other, sketch)


def bases_kernel(place_ref, rows_ref, parts_ref, *refs):
    out_ref = refs[-1]
    rows = rows_ref[...].reshape(-1, rows_ref.shape[-1])
    out_ref[...] = (
        lax.dot_general(
            jnp.concatenate([rows, rows], axis=1), parts_ref[...], NT, preferred_element_type=F32
        )
        .astype(BF16)
        .reshape(out_ref.shape)
    )


def bases(place, rows, parts, other, before=None):
    sources, height, rank = rows.shape
    tile = 16
    args = (place, rows, parts)
    in_specs = [
        pl.BlockSpec((tile, height, rank), lambda i, p: (i, 0, 0)),
        pl.BlockSpec(parts.shape, lambda i, p: (0, 0)),
    ]
    aliases = {}
    if before is not None:
        args += (before,)
        in_specs.append(pl.BlockSpec(memory_space=pl.ANY))
        aliases = {3: 0}
    total = sources * height
    return pl.pallas_call(
        bases_kernel,
        out_shape=jax.ShapeDtypeStruct((sources, 2, height, rank), BF16),
        grid_spec=pltpu.PrefetchScalarGridSpec(
            num_scalar_prefetch=1,
            grid=(sources // tile,),
            in_specs=in_specs,
            out_specs=pl.BlockSpec(
                (tile, 1, height, rank), lambda i, p: (i, p[2] ^ other, 0, 0)
            ),
        ),
        input_output_aliases=aliases,
        compiler_params=pltpu.CompilerParams(vmem_limit_bytes=32 * 2**20),
        cost_estimate=pl.CostEstimate(
            flops=4 * total * rank * rank, bytes_accessed=4 * total * rank, transcendentals=0
        ),
        name="bases",
    )(*args)


def shift(value, axis, distance):
    size = lax.axis_size(axis)
    return lax.ppermute(value, axis, [(i, (i + distance) % size) for i in range(size)])


def swap(value, axis, mask):
    return lax.ppermute(value, axis, [(i, i ^ mask) for i in range(lax.axis_size(axis))])


def ring_sends(term):
    return term(3, 2), term(5, 2)


def ring_finish(term, sends, axis):
    up = shift(sends[0], axis, 1)
    down = shift(sends[1], axis, -1)
    up_last = shift(term(2, 1) + up[1:], axis, 1)
    down_last = shift(term(7, 1) + down[:1], axis, -1)
    own = term(0, 2)
    return own[0] + down[1] + up_last[0], own[1] + up[0] + down_last[0]


def scatter_ring(term, axis):
    return ring_finish(term, ring_sends(term), axis)


def body(samples, row_order, cluster_map, leaf_sketch, level_sketch):
    place = jnp.stack([lax.axis_index(a) for a in ("z", "y", "core", "x")]).astype(jnp.int32)
    rows = row_order.shape[1]
    rank = leaf_sketch.shape[1]
    row_norm = float(lax.axis_size("x") * samples.shape[0])
    first, second, send_a, send_b, keep_a, keep_b = prepare(
        samples, row_order, cluster_map, leaf_sketch, place
    )

    def to_cluster(packed):
        packed = packed.reshape(-1, 2 * rows, rank)
        return lax.all_to_all(packed, ("z", "y"), split_axis=0, concat_axis=0, tiled=True)

    got_b = swap(send_b, "core", 1)
    got_a = swap(send_a, "core", 1)
    second = swap(second, "core", 1)
    keep_a, got_a = (v.reshape(8, 2, 8, -1, v.shape[-1]) for v in (keep_a, got_a))
    keep_b, got_b = (v.reshape(8, 2, 8, -1, v.shape[-1]) for v in (keep_b, got_b))
    term_a = lambda i, n: keep_a[i : i + n] + got_a[i : i + n]
    term_b = lambda i, n: keep_b[i : i + n] + got_b[i : i + n]
    sends_a, first = lax.optimization_barrier((ring_sends(term_a), first))
    low_b, high_b = ring_finish(term_b, ring_sends(term_b), "y")
    low_a, high_a = ring_finish(term_a, sends_a, "x")
    first = to_cluster(first)
    part_a = jnp.concatenate([low_a, high_a], axis=0).reshape(8, 4, -1, low_a.shape[-1])
    part_b = jnp.concatenate([low_b, high_b], axis=0).reshape(8, 4, -1, low_b.shape[-1])
    low_a, high_a = scatter_ring(lambda i, n: part_a[i : i + n], "y")
    low_b, high_b = scatter_ring(lambda i, n: part_b[i : i + n], "x")
    part_a = jnp.concatenate([low_a, high_a], axis=0)
    part_b = jnp.concatenate([low_b, high_b], axis=0)
    total = jnp.concatenate([part_a, part_b], axis=1)
    for mask in (1, 2, 4):
        half = total.shape[0] // 2
        total = total[:half] + swap(total[half:], "z", mask)
    second, total = lax.optimization_barrier((second, total))
    second = to_cluster(second)
    near = swap(total, "x", 1)
    far = swap(jnp.concatenate([total, near], axis=0), "x", 2)
    parts, node = leaf_node(place, (total[0], near[0], far), leaf_sketch, row_norm)
    halves = []
    for depth, (axis, bit) in enumerate((("core", 1), ("y", 1), ("y", 2))):
        other = swap(node, axis, bit)
        if depth == 1:
            basis, other = lax.optimization_barrier((bases(place, first, parts, 0), other))
        half, node = merge(node, other, level_sketch[depth])
        halves.append(half)
    basis = bases(place, second, parts, 1, basis).reshape(-1, rank)
    return (basis, jnp.stack(halves, axis=0)[None], node[None])


def solution(mesh):
    grid = Mesh(mesh.devices.reshape(8, 4, 2, 4), ("z", "y", "core", "x"))
    every = ("z", "y", "core", "x")
    leaf = ("z", "y", "core")
    in_specs = (P(every, None), P(every, None), P(every), P(), P())
    out_specs = (P(every, None), P(leaf, None, None, None), P(leaf, None, None))
    return jax.shard_map(body, mesh=grid, in_specs=in_specs, out_specs=out_specs, check_vma=False)
```

```python
import functools
import math

import jax
import jax.numpy as jnp
from jax import lax
from jax.experimental import pallas as pl
from jax.experimental.pallas import tpu as pltpu
from jax.sharding import Mesh, PartitionSpec as P

LEVELS = 3
SHIFT = 0.01
PANEL = 32
HIGHEST = lax.Precision.HIGHEST
F32 = jnp.float32
BF16 = jnp.bfloat16
VMEM_LIMIT = 56 * 2**20

NT = (((1,), (1,)), ((), ()))
TN = (((0,), (0,)), ((), ()))


def exact(a, b, dims=(((1,), (0,)), ((), ()))):
    return lax.dot_general(a, b, dims, precision=HIGHEST, preferred_element_type=F32)


def cholesky_inverse(work, inverse):
    n = inverse.shape[0]
    row = lax.broadcasted_iota(jnp.int32, (PANEL, n), 0)
    for first in range(0, n, PANEL):
        left = work[first : first + PANEL, :n]
        right = work[first : first + PANEL, n:]
        cols = [
            jnp.broadcast_to(left[:, first + j : first + j + 1], (PANEL, n)) for j in range(PANEL)
        ]
        scale = jnp.zeros((PANEL, n), F32)
        for j in range(PANEL):
            pivot = cols[j][j : j + 1]
            factor = jnp.where(row > j, cols[j] * (1.0 / pivot), 0.0)
            scale = jnp.where(row == j, lax.rsqrt(pivot), scale)
            left = left - factor * left[j : j + 1]
            right = right - factor * right[j : j + 1]
            for k in range(j + 1, PANEL):
                cols[k] = cols[k] - factor * cols[k][j : j + 1]
        left = left * scale
        right = right * scale
        inverse[first : first + PANEL, :] = right
        rest = first + PANEL
        if rest < n:
            both = jnp.concatenate([left, right], axis=1)
            update = exact(left, both, TN)
            work[rest:, :] = work[rest:, :] - update[rest:, :]


def identity(n):
    shape = (n, n)
    return (
        lax.broadcasted_iota(jnp.int32, shape, 0) == lax.broadcasted_iota(jnp.int32, shape, 1)
    ).astype(F32)


def prep_kernel(
    map_ref, place_ref, order_ref, samples_hbm, sketch_ref,
    first_ref, second_ref, send_a, send_b, keep_a, keep_b,
    parts, ordered, slots, count, columns, samples_ref, arrived,
):
    blocks, rows, width = samples_ref.shape
    zs, ys, cores, xs = 8, 4, 2, 4
    rank = sketch_ref.shape[1]
    group = columns.shape[0]
    each = blocks // group
    step = pl.program_id(0)

    def load(g):
        some = pl.ds(g * each, each)
        return pltpu.make_async_copy(samples_hbm.at[some], samples_ref.at[some], arrived.at[g])

    @pl.when(step == 0)
    def _():
        for g in range(group):
            load(g).start()
        clusters = count.shape[0]

        def clear(c, _):
            count[c] = 0
            slots[2 * c] = blocks
            slots[2 * c + 1] = blocks
            return 0

        lax.fori_loop(0, clusters, clear, 0)

        def place(b, _):
            c = map_ref[b]
            slots[2 * c + count[c]] = b
            count[c] = count[c] + 1
            return 0

        lax.fori_loop(0, blocks, place, 0)
        parts[blocks] = jnp.zeros((2 * rank, rows), BF16)
        ordered[blocks] = jnp.zeros((rows, rank), BF16)
        turned = order_ref[...].astype(F32).T
        for g in range(group):
            columns[g] = turned[:, g * each : (g + 1) * each]
        sketch_t = sketch_ref[...].astype(F32).T.astype(BF16)
        lane = lax.broadcasted_iota(jnp.int32, (rows, rows), 1).astype(F32)

        def some(g, _):
            load(g).wait()
            column = columns[g]
            for u in range(each):
                b = g * each + u
                value = lax.dot_general(
                    sketch_t, samples_ref[b], NT, preferred_element_type=F32
                )
                high = value.astype(BF16)
                low = (value - high.astype(F32)).astype(BF16)
                parts[b, :rank, :] = high
                parts[b, rank:, :] = low
                pick = (jnp.broadcast_to(column[:, u : u + 1], (rows, rows)) == lane).astype(F32)
                ordered[b] = lax.dot_general(
                    pick.astype(BF16), high, NT, preferred_element_type=F32
                ).astype(BF16)
            return 0

        lax.fori_loop(0, group, some, 0)

    my_z, my_y, my_core, my_x = (place_ref[i] for i in range(4))
    y = lax.rem(my_y + step, ys)
    quarter = rows // 2 // xs

    def one(z_rel, _):
        flip = ((z_rel & 1) << 2) | (z_rel & 2) | (z_rel >> 2)
        z = my_z ^ flip
        for k_rel, out_a, out_b in ((0, keep_a, keep_b), (1, send_a, send_b)):
            core = my_core if k_rel == 0 else 1 - my_core
            cluster = (z * ys + y) * cores + core
            b0 = slots[2 * cluster]
            b1 = slots[2 * cluster + 1]
            out = first_ref if k_rel == 0 else second_ref
            out[z, 0, :rows] = ordered[b0]
            out[z, 0, rows:] = ordered[b1]
            lhs = jnp.concatenate([parts[b0], parts[b1]], axis=1)
            rhs = jnp.concatenate(
                [samples_ref[jnp.minimum(b0, blocks - 1)], samples_ref[jnp.minimum(b1, blocks - 1)]],
                axis=0,
            )
            both = jnp.dot(lhs, rhs, preferred_element_type=F32)
            total = both[:rank] + both[rank:]
            for x in range(xs):
                x_rel = lax.rem(x - my_x + xs, xs)
                out_a[x_rel, 0, 0, z_rel] = total[x * quarter : (x + 1) * quarter]
                out_b[0, x_rel, z_rel] = total[rank // 2 + x * quarter : rank // 2 + (x + 1) * quarter]
        return 0

    lax.fori_loop(0, zs, one, 0, unroll=8)


def prepare(samples, row_order, cluster_map, leaf_sketch, place):
    blocks, rows = row_order.shape
    width = samples.shape[1]
    rank = leaf_sketch.shape[1]
    samples = samples.reshape(blocks, rows, width)
    zs, ys, cores, xs = 8, 4, 2, 4
    quarter = rows // 2 // xs
    chunk_a = jax.ShapeDtypeStruct((xs, 2, ys // 2, zs, quarter, width), F32)
    chunk_b = jax.ShapeDtypeStruct((ys, xs, zs, quarter, width), F32)
    spec_a = pl.BlockSpec((xs, 1, 1, zs, quarter, width), lambda i, m, p: (0, i // 2, i % 2, 0, 0, 0))
    spec_b = pl.BlockSpec((1, xs, zs, quarter, width), lambda i, m, p: (i, 0, 0, 0, 0))
    packed = jax.ShapeDtypeStruct((zs, ys, 2 * rows, rank), BF16)
    packed_spec = pl.BlockSpec(
        (zs, 1, 2 * rows, rank), lambda i, m, p: (0, lax.rem(p[1] + i, 4), 0, 0)
    )
    return pl.pallas_call(
        prep_kernel,
        out_shape=(packed, packed, chunk_a, chunk_b, chunk_a, chunk_b),
        grid_spec=pltpu.PrefetchScalarGridSpec(
            num_scalar_prefetch=2,
            grid=(ys,),
            in_specs=[
                pl.BlockSpec(row_order.shape, lambda i, m, p: (0, 0)),
                pl.BlockSpec(memory_space=pl.ANY),
                pl.BlockSpec(leaf_sketch.shape, lambda i, m, p: (0, 0)),
            ],
            out_specs=[packed_spec, packed_spec, spec_a, spec_b, spec_a, spec_b],
            scratch_shapes=[
                pltpu.VMEM((blocks + 1, 2 * rank, rows), BF16),
                pltpu.VMEM((blocks + 1, rows, rank), BF16),
                pltpu.SMEM((2 * zs * ys * cores,), jnp.int32),
                pltpu.SMEM((zs * ys * cores,), jnp.int32),
                pltpu.VMEM((8, rows, blocks // 8), F32),
                pltpu.VMEM(samples.shape, BF16),
                pltpu.SemaphoreType.DMA((8,)),
            ],
        ),
        compiler_params=pltpu.CompilerParams(vmem_limit_bytes=VMEM_LIMIT),
        cost_estimate=pl.CostEstimate(
            flops=6 * 10**9, bytes_accessed=16 * 2**20, transcendentals=0
        ),
        name="prepare",
    )(cluster_map, place, row_order, samples, leaf_sketch)


def leaf_kernel(row_norm, place_ref, c0, c1, c2, sketch_ref, parts_ref, node_ref, cross, work, inverse):
    rank, width = node_ref.shape
    quarter = rank // 8
    my_x = place_ref[3]
    for rel, chunk in enumerate((c0, c1, c2.at[0], c2.at[1])):
        start = pl.multiple_of((my_x ^ rel) * quarter, quarter)
        cross[pl.ds(start, quarter), :] = chunk[:quarter, :]
        cross[pl.ds(start + rank // 2, quarter), :] = chunk[quarter:, :]
    eye = identity(rank)
    gram = exact(cross[...], sketch_ref[...].astype(F32)) / row_norm + SHIFT * eye
    work[:, :rank] = gram
    work[:, rank:] = eye
    cholesky_inverse(work, inverse)
    whole = inverse[...]
    high = whole.astype(BF16)
    parts_ref[:, :rank] = high
    parts_ref[:, rank:] = (whole - high.astype(F32)).astype(BF16)
    node_ref[...] = exact(whole, cross[...]) * (math.sqrt(width) / row_norm)


def leaf_node(place, chunks, leaf_sketch, row_norm):
    rank = leaf_sketch.shape[1]
    width = leaf_sketch.shape[0]
    vmem = pl.BlockSpec(memory_space=pltpu.VMEM)
    return pl.pallas_call(
        functools.partial(leaf_kernel, row_norm),
        out_shape=(
            jax.ShapeDtypeStruct((rank, 2 * rank), BF16),
            jax.ShapeDtypeStruct((rank, width), F32),
        ),
        in_specs=[pl.BlockSpec(memory_space=pltpu.SMEM)] + [vmem] * 4,
        out_specs=(vmem, vmem),
        scratch_shapes=[
            pltpu.VMEM((rank, width), F32),
            pltpu.VMEM((rank, 2 * rank), F32),
            pltpu.VMEM((rank, rank), F32),
        ],
        compiler_params=pltpu.CompilerParams(vmem_limit_bytes=16 * 2**20),
        cost_estimate=pl.CostEstimate(flops=8*10**9, bytes_accessed=2**16, transcendentals=0),
        name="leaf_node",
    )(place, *chunks, leaf_sketch)


def merge_kernel(own_ref, other_ref, sketch_ref, transfer_ref, node_ref, work, inverse):
    rank, width = node_ref.shape
    total = 2.0 * rank
    sketch = sketch_ref[...]
    own, other = own_ref[...], other_ref[...]
    own_z = exact(own, sketch)
    other_z = exact(other, sketch)
    z = jnp.concatenate([own_z, other_z], axis=0)
    stacked = jnp.concatenate([own, other], axis=0)
    z_t = z.T
    gram = exact(z_t, z) / total
    product = exact(z_t, stacked)
    eye = identity(rank)
    work[:, :rank] = gram + SHIFT * eye
    work[:, rank:] = eye
    cholesky_inverse(work, inverse)
    whole = inverse[...]
    node_ref[...] = exact(whole, product) * (math.sqrt(width) / total)
    transfer_ref[...] = exact(own_z, whole, NT)


def merge(own, other, sketch):
    rank, width = own.shape
    vmem = pl.BlockSpec(memory_space=pltpu.VMEM)
    return pl.pallas_call(
        merge_kernel,
        out_shape=(
            jax.ShapeDtypeStruct((rank, rank), F32),
            jax.ShapeDtypeStruct((rank, width), F32),
        ),
        in_specs=[vmem] * 3,
        out_specs=(vmem, vmem),
        scratch_shapes=[pltpu.VMEM((rank, 2 * rank), F32), pltpu.VMEM((rank, rank), F32)],
        compiler_params=pltpu.CompilerParams(vmem_limit_bytes=16 * 2**20),
        cost_estimate=pl.CostEstimate(flops=8*10**9, bytes_accessed=2**16, transcendentals=0),
        name="merge",
    )(own, other, sketch)


def bases_kernel(place_ref, rows_ref, parts_ref, *refs):
    out_ref = refs[-1]
    rows = rows_ref[...].reshape(-1, rows_ref.shape[-1])
    out_ref[...] = (
        lax.dot_general(
            jnp.concatenate([rows, rows], axis=1), parts_ref[...], NT, preferred_element_type=F32
        )
        .astype(BF16)
        .reshape(out_ref.shape)
    )


def bases(place, rows, parts, other, before=None):
    sources, height, rank = rows.shape
    tile = 16
    args = (place, rows, parts)
    in_specs = [
        pl.BlockSpec((tile, height, rank), lambda i, p: (i, 0, 0)),
        pl.BlockSpec(parts.shape, lambda i, p: (0, 0)),
    ]
    aliases = {}
    if before is not None:
        args += (before,)
        in_specs.append(pl.BlockSpec(memory_space=pl.ANY))
        aliases = {3: 0}
    total = sources * height
    return pl.pallas_call(
        bases_kernel,
        out_shape=jax.ShapeDtypeStruct((sources, 2, height, rank), BF16),
        grid_spec=pltpu.PrefetchScalarGridSpec(
            num_scalar_prefetch=1,
            grid=(sources // tile,),
            in_specs=in_specs,
            out_specs=pl.BlockSpec(
                (tile, 1, height, rank), lambda i, p: (i, p[2] ^ other, 0, 0)
            ),
        ),
        input_output_aliases=aliases,
        compiler_params=pltpu.CompilerParams(vmem_limit_bytes=32 * 2**20),
        cost_estimate=pl.CostEstimate(
            flops=4 * total * rank * rank, bytes_accessed=4 * total * rank, transcendentals=0
        ),
        name="bases",
    )(*args)


def shift(value, axis, distance):
    size = lax.axis_size(axis)
    return lax.ppermute(value, axis, [(i, (i + distance) % size) for i in range(size)])


def swap(value, axis, mask):
    return lax.ppermute(value, axis, [(i, i ^ mask) for i in range(lax.axis_size(axis))])


def ring_sends(term):
    return term(3, 2), term(5, 2)


def ring_finish(term, sends, axis, tied=None):
    up = shift(sends[0], axis, 1)
    down = shift(sends[1], axis, -1)
    if tied is not None:
        up, down, tied = lax.optimization_barrier((up, down, tied))
    up_last = shift(term(2, 1) + up[1:], axis, 1)
    down_last = shift(term(7, 1) + down[:1], axis, -1)
    own = term(0, 2)
    return own[0] + down[1] + up_last[0], own[1] + up[0] + down_last[0], tied


def scatter_ring(term, axis):
    return ring_finish(term, ring_sends(term), axis)[:2]


def body(samples, row_order, cluster_map, leaf_sketch, level_sketch):
    place = jnp.stack([lax.axis_index(a) for a in ("z", "y", "core", "x")]).astype(jnp.int32)
    rows = row_order.shape[1]
    rank = leaf_sketch.shape[1]
    row_norm = float(lax.axis_size("x") * samples.shape[0])
    first, second, send_a, send_b, keep_a, keep_b = prepare(
        samples, row_order, cluster_map, leaf_sketch, place
    )

    def to_cluster(packed):
        packed = packed.reshape(-1, 2 * rows, rank)
        return lax.all_to_all(packed, ("z", "y"), split_axis=0, concat_axis=0, tiled=True)

    got_b = swap(send_b, "core", 1)
    send_a, got_b = lax.optimization_barrier((send_a, got_b))
    got_a = swap(send_a, "core", 1)
    second = swap(second, "core", 1)
    keep_a, got_a = (v.reshape(8, 2, 8, -1, v.shape[-1]) for v in (keep_a, got_a))
    keep_b, got_b = (v.reshape(8, 2, 8, -1, v.shape[-1]) for v in (keep_b, got_b))
    term_a = lambda i, n: keep_a[i : i + n] + got_a[i : i + n]
    term_b = lambda i, n: keep_b[i : i + n] + got_b[i : i + n]
    sends_b, first = lax.optimization_barrier((ring_sends(term_b), first))
    low_b, high_b, sends_a = ring_finish(term_b, sends_b, "y", ring_sends(term_a))
    low_a, high_a, _ = ring_finish(term_a, sends_a, "x")
    first = to_cluster(first)
    part_a = jnp.concatenate([low_a, high_a], axis=0).reshape(8, 4, -1, low_a.shape[-1])
    part_b = jnp.concatenate([low_b, high_b], axis=0).reshape(8, 4, -1, low_b.shape[-1])
    low_a, high_a = scatter_ring(lambda i, n: part_a[i : i + n], "y")
    low_b, high_b = scatter_ring(lambda i, n: part_b[i : i + n], "x")
    part_a = jnp.concatenate([low_a, high_a], axis=0)
    part_b = jnp.concatenate([low_b, high_b], axis=0)
    total = jnp.concatenate([part_a, part_b], axis=1)
    for mask in (1, 2, 4):
        half = total.shape[0] // 2
        if half == 1:
            second, total, first = lax.optimization_barrier((second, total, first))
        total = total[:half] + swap(total[half:], "z", mask)
    second = to_cluster(second)
    near = swap(total, "x", 1)
    far = swap(jnp.concatenate([total, near], axis=0), "x", 2)
    parts, node = leaf_node(place, (total[0], near[0], far), leaf_sketch, row_norm)
    halves = []
    for depth, (axis, bit) in enumerate((("core", 1), ("y", 1), ("y", 2))):
        other = swap(node, axis, bit)
        if depth == 1:
            basis, other = lax.optimization_barrier((bases(place, first, parts, 0), other))
        half, node = merge(node, other, level_sketch[depth])
        halves.append(half)
    basis = bases(place, second, parts, 1, basis).reshape(-1, rank)
    return (basis, jnp.stack(halves, axis=0)[None], node[None])


def solution(mesh):
    grid = Mesh(mesh.devices.reshape(8, 4, 2, 4), ("z", "y", "core", "x"))
    every = ("z", "y", "core", "x")
    leaf = ("z", "y", "core")
    in_specs = (P(every, None), P(every, None), P(every), P(), P())
    out_specs = (P(every, None), P(leaf, None, None, None), P(leaf, None, None))
    return jax.shard_map(body, mesh=grid, in_specs=in_specs, out_specs=out_specs, check_vma=False)
```

```python
import functools
import math

import jax
import jax.numpy as jnp
from jax import lax
from jax.experimental import pallas as pl
from jax.experimental.pallas import tpu as pltpu
from jax.sharding import Mesh, PartitionSpec as P

LEVELS = 3
SHIFT = 0.01
PANEL = 32
HIGHEST = lax.Precision.HIGHEST
F32 = jnp.float32
BF16 = jnp.bfloat16
VMEM_LIMIT = 56 * 2**20

NT = (((1,), (1,)), ((), ()))
TN = (((0,), (0,)), ((), ()))


def exact(a, b, dims=(((1,), (0,)), ((), ()))):
    return lax.dot_general(a, b, dims, precision=HIGHEST, preferred_element_type=F32)


def cholesky_inverse(work, inverse):
    n = inverse.shape[0]
    row = lax.broadcasted_iota(jnp.int32, (PANEL, n), 0)
    for first in range(0, n, PANEL):
        left = work[first : first + PANEL, :n]
        right = work[first : first + PANEL, n:]
        cols = [
            jnp.broadcast_to(left[:, first + j : first + j + 1], (PANEL, n)) for j in range(PANEL)
        ]
        scale = jnp.zeros((PANEL, n), F32)
        for j in range(PANEL):
            pivot = cols[j][j : j + 1]
            factor = jnp.where(row > j, cols[j] * (1.0 / pivot), 0.0)
            scale = jnp.where(row == j, lax.rsqrt(pivot), scale)
            left = left - factor * left[j : j + 1]
            right = right - factor * right[j : j + 1]
            for k in range(j + 1, PANEL):
                cols[k] = cols[k] - factor * cols[k][j : j + 1]
        left = left * scale
        right = right * scale
        inverse[first : first + PANEL, :] = right
        rest = first + PANEL
        if rest < n:
            both = jnp.concatenate([left, right], axis=1)
            update = exact(left, both, TN)
            work[rest:, :] = work[rest:, :] - update[rest:, :]


def identity(n):
    shape = (n, n)
    return (
        lax.broadcasted_iota(jnp.int32, shape, 0) == lax.broadcasted_iota(jnp.int32, shape, 1)
    ).astype(F32)


def prep_kernel(
    map_ref, place_ref, order_ref, samples_hbm, sketch_ref,
    first_ref, second_ref, send_a, send_b, keep_a, keep_b,
    parts, ordered, slots, count, columns, samples_ref, arrived,
):
    blocks, rows, width = samples_ref.shape
    zs, ys, cores, xs = 8, 4, 2, 4
    rank = sketch_ref.shape[1]
    group = columns.shape[0]
    each = blocks // group
    step = pl.program_id(0)

    def load(g):
        some = pl.ds(g * each, each)
        return pltpu.make_async_copy(samples_hbm.at[some], samples_ref.at[some], arrived.at[g])

    @pl.when(step == 0)
    def _():
        for g in range(group):
            load(g).start()
        clusters = count.shape[0]

        def clear(c, _):
            count[c] = 0
            slots[2 * c] = blocks
            slots[2 * c + 1] = blocks
            return 0

        lax.fori_loop(0, clusters, clear, 0)

        def place(b, _):
            c = map_ref[b]
            slots[2 * c + count[c]] = b
            count[c] = count[c] + 1
            return 0

        lax.fori_loop(0, blocks, place, 0)
        parts[blocks] = jnp.zeros((2 * rank, rows), BF16)
        ordered[blocks] = jnp.zeros((rows, rank), BF16)
        turned = order_ref[...].astype(F32).T
        for g in range(group):
            columns[g] = turned[:, g * each : (g + 1) * each]
        sketch_t = sketch_ref[...].astype(F32).T.astype(BF16)
        lane = lax.broadcasted_iota(jnp.int32, (rows, rows), 1).astype(F32)

        def some(g, _):
            load(g).wait()
            column = columns[g]
            for u in range(each):
                b = g * each + u
                value = lax.dot_general(
                    sketch_t, samples_ref[b], NT, preferred_element_type=F32
                )
                high = value.astype(BF16)
                low = (value - high.astype(F32)).astype(BF16)
                parts[b, :rank, :] = high
                parts[b, rank:, :] = low
                pick = (jnp.broadcast_to(column[:, u : u + 1], (rows, rows)) == lane).astype(F32)
                ordered[b] = lax.dot_general(
                    pick.astype(BF16), high, NT, preferred_element_type=F32
                ).astype(BF16)
            return 0

        lax.fori_loop(0, group, some, 0)

    my_z, my_y, my_core, my_x = (place_ref[i] for i in range(4))
    y = lax.rem(my_y + step, ys)
    quarter = rows // 2 // xs

    def one(z_rel, _):
        flip = ((z_rel & 1) << 2) | (z_rel & 2) | (z_rel >> 2)
        z = my_z ^ flip
        for k_rel, out_a, out_b in ((0, keep_a, keep_b), (1, send_a, send_b)):
            core = my_core if k_rel == 0 else 1 - my_core
            cluster = (z * ys + y) * cores + core
            b0 = slots[2 * cluster]
            b1 = slots[2 * cluster + 1]
            out = first_ref if k_rel == 0 else second_ref
            out[z, 0, :rows] = ordered[b0]
            out[z, 0, rows:] = ordered[b1]
            lhs = jnp.concatenate([parts[b0], parts[b1]], axis=1)
            rhs = jnp.concatenate(
                [samples_ref[jnp.minimum(b0, blocks - 1)], samples_ref[jnp.minimum(b1, blocks - 1)]],
                axis=0,
            )
            both = jnp.dot(lhs, rhs, preferred_element_type=F32)
            total = both[:rank] + both[rank:]
            for x in range(xs):
                x_rel = lax.rem(x - my_x + xs, xs)
                out_a[x_rel, 0, 0, z_rel] = total[x * quarter : (x + 1) * quarter]
                out_b[0, x_rel, z_rel] = total[rank // 2 + x * quarter : rank // 2 + (x + 1) * quarter]
        return 0

    lax.fori_loop(0, zs, one, 0, unroll=8)


def prepare(samples, row_order, cluster_map, leaf_sketch, place):
    blocks, rows = row_order.shape
    width = samples.shape[1]
    rank = leaf_sketch.shape[1]
    samples = samples.reshape(blocks, rows, width)
    zs, ys, cores, xs = 8, 4, 2, 4
    quarter = rows // 2 // xs
    chunk_a = jax.ShapeDtypeStruct((xs, 2, ys // 2, zs, quarter, width), F32)
    chunk_b = jax.ShapeDtypeStruct((ys, xs, zs, quarter, width), F32)
    spec_a = pl.BlockSpec((xs, 1, 1, zs, quarter, width), lambda i, m, p: (0, i // 2, i % 2, 0, 0, 0))
    spec_b = pl.BlockSpec((1, xs, zs, quarter, width), lambda i, m, p: (i, 0, 0, 0, 0))
    packed = jax.ShapeDtypeStruct((zs, ys, 2 * rows, rank), BF16)
    packed_spec = pl.BlockSpec(
        (zs, 1, 2 * rows, rank), lambda i, m, p: (0, lax.rem(p[1] + i, 4), 0, 0)
    )
    return pl.pallas_call(
        prep_kernel,
        out_shape=(packed, packed, chunk_a, chunk_b, chunk_a, chunk_b),
        grid_spec=pltpu.PrefetchScalarGridSpec(
            num_scalar_prefetch=2,
            grid=(ys,),
            in_specs=[
                pl.BlockSpec(row_order.shape, lambda i, m, p: (0, 0)),
                pl.BlockSpec(memory_space=pl.ANY),
                pl.BlockSpec(leaf_sketch.shape, lambda i, m, p: (0, 0)),
            ],
            out_specs=[packed_spec, packed_spec, spec_a, spec_b, spec_a, spec_b],
            scratch_shapes=[
                pltpu.VMEM((blocks + 1, 2 * rank, rows), BF16),
                pltpu.VMEM((blocks + 1, rows, rank), BF16),
                pltpu.SMEM((2 * zs * ys * cores,), jnp.int32),
                pltpu.SMEM((zs * ys * cores,), jnp.int32),
                pltpu.VMEM((8, rows, blocks // 8), F32),
                pltpu.VMEM(samples.shape, BF16),
                pltpu.SemaphoreType.DMA((8,)),
            ],
        ),
        compiler_params=pltpu.CompilerParams(vmem_limit_bytes=VMEM_LIMIT),
        cost_estimate=pl.CostEstimate(
            flops=6 * 10**9, bytes_accessed=16 * 2**20, transcendentals=0
        ),
        name="prepare",
    )(cluster_map, place, row_order, samples, leaf_sketch)


def leaf_kernel(row_norm, place_ref, c0, c1, c2, c3, sketch_ref, parts_ref, node_ref, cross, work, inverse):
    rank, width = node_ref.shape
    quarter = rank // 8
    my_x = place_ref[3]
    for rel, chunk in enumerate((c0, c1, c2, c3)):
        start = pl.multiple_of((my_x ^ rel) * quarter, quarter)
        cross[pl.ds(start, quarter), :] = chunk[:quarter, :]
        cross[pl.ds(start + rank // 2, quarter), :] = chunk[quarter:, :]
    eye = identity(rank)
    gram = exact(cross[...], sketch_ref[...].astype(F32)) / row_norm + SHIFT * eye
    work[:, :rank] = gram
    work[:, rank:] = eye
    cholesky_inverse(work, inverse)
    whole = inverse[...]
    high = whole.astype(BF16)
    parts_ref[:, :rank] = high
    parts_ref[:, rank:] = (whole - high.astype(F32)).astype(BF16)
    node_ref[...] = exact(whole, cross[...]) * (math.sqrt(width) / row_norm)


def leaf_node(place, chunks, leaf_sketch, row_norm):
    rank = leaf_sketch.shape[1]
    width = leaf_sketch.shape[0]
    vmem = pl.BlockSpec(memory_space=pltpu.VMEM)
    return pl.pallas_call(
        functools.partial(leaf_kernel, row_norm),
        out_shape=(
            jax.ShapeDtypeStruct((rank, 2 * rank), BF16),
            jax.ShapeDtypeStruct((rank, width), F32),
        ),
        in_specs=[pl.BlockSpec(memory_space=pltpu.SMEM)] + [vmem] * 5,
        out_specs=(vmem, vmem),
        scratch_shapes=[
            pltpu.VMEM((rank, width), F32),
            pltpu.VMEM((rank, 2 * rank), F32),
            pltpu.VMEM((rank, rank), F32),
        ],
        compiler_params=pltpu.CompilerParams(vmem_limit_bytes=16 * 2**20),
        cost_estimate=pl.CostEstimate(flops=9*10**9, bytes_accessed=2**16, transcendentals=0),
        name="leaf_node",
    )(place, *chunks, leaf_sketch)


def merge_kernel(own_ref, other_ref, sketch_ref, *refs):
    *earlier, transfer_ref, node_ref, work, inverse = refs
    for i, half in enumerate(earlier):
        transfer_ref[i] = half[0]
    rank, width = node_ref.shape
    total = 2.0 * rank
    sketch = sketch_ref[...]
    own, other = own_ref[...], other_ref[...]
    own_z = exact(own, sketch)
    other_z = exact(other, sketch)
    z = jnp.concatenate([own_z, other_z], axis=0)
    stacked = jnp.concatenate([own, other], axis=0)
    z_t = z.T
    gram = exact(z_t, z) / total
    product = exact(z_t, stacked)
    eye = identity(rank)
    work[:, :rank] = gram + SHIFT * eye
    work[:, rank:] = eye
    cholesky_inverse(work, inverse)
    whole = inverse[...]
    node_ref[...] = exact(whole, product) * (math.sqrt(width) / total)
    transfer_ref[len(earlier)] = exact(own_z, whole, NT)


def merge(own, other, sketch, earlier=()):
    rank, width = own.shape
    vmem = pl.BlockSpec(memory_space=pltpu.VMEM)
    return pl.pallas_call(
        merge_kernel,
        out_shape=(
            jax.ShapeDtypeStruct((len(earlier) + 1, rank, rank), F32),
            jax.ShapeDtypeStruct((rank, width), F32),
        ),
        in_specs=[vmem] * (3 + len(earlier)),
        out_specs=(vmem, vmem),
        scratch_shapes=[pltpu.VMEM((rank, 2 * rank), F32), pltpu.VMEM((rank, rank), F32)],
        compiler_params=pltpu.CompilerParams(vmem_limit_bytes=16 * 2**20),
        cost_estimate=pl.CostEstimate(flops=9*10**9, bytes_accessed=2**16, transcendentals=0),
        name="merge",
    )(own, other, sketch, *earlier)


def bases_kernel(place_ref, rows_ref, parts_ref, *refs):
    out_ref = refs[-1]
    rows = rows_ref[...].reshape(-1, rows_ref.shape[-1])
    out_ref[...] = (
        lax.dot_general(
            jnp.concatenate([rows, rows], axis=1), parts_ref[...], NT, preferred_element_type=F32
        )
        .astype(BF16)
        .reshape(out_ref.shape)
    )


def bases(place, rows, parts, other, before=None):
    sources, height, rank = rows.shape
    tile = 16
    args = (place, rows, parts)
    in_specs = [
        pl.BlockSpec((tile, height, rank), lambda i, p: (i, 0, 0)),
        pl.BlockSpec(parts.shape, lambda i, p: (0, 0)),
    ]
    aliases = {}
    if before is not None:
        args += (before,)
        in_specs.append(pl.BlockSpec(memory_space=pl.ANY))
        aliases = {3: 0}
    total = sources * height
    return pl.pallas_call(
        bases_kernel,
        out_shape=jax.ShapeDtypeStruct((sources, 2, height, rank), BF16),
        grid_spec=pltpu.PrefetchScalarGridSpec(
            num_scalar_prefetch=1,
            grid=(sources // tile,),
            in_specs=in_specs,
            out_specs=pl.BlockSpec(
                (tile, 1, height, rank), lambda i, p: (i, p[2] ^ other, 0, 0)
            ),
        ),
        input_output_aliases=aliases,
        compiler_params=pltpu.CompilerParams(vmem_limit_bytes=32 * 2**20),
        cost_estimate=pl.CostEstimate(
            flops=4 * total * rank * rank, bytes_accessed=4 * total * rank, transcendentals=0
        ),
        name="bases",
    )(*args)


def shift(value, axis, distance):
    size = lax.axis_size(axis)
    return lax.ppermute(value, axis, [(i, (i + distance) % size) for i in range(size)])


def swap(value, axis, mask):
    return lax.ppermute(value, axis, [(i, i ^ mask) for i in range(lax.axis_size(axis))])


def ring_sends(term):
    return term(3, 2), term(5, 2)


def ring_finish(term, sends, axis, tied=None):
    up = shift(sends[0], axis, 1)
    down = shift(sends[1], axis, -1)
    if tied is not None:
        up, down, tied = lax.optimization_barrier((up, down, tied))
    up_last = shift(term(2, 1) + up[1:], axis, 1)
    down_last = shift(term(7, 1) + down[:1], axis, -1)
    own = term(0, 2)
    return own[0] + down[1] + up_last[0], own[1] + up[0] + down_last[0], tied


def scatter_ring(term, axis):
    return ring_finish(term, ring_sends(term), axis)[:2]


def body(samples, row_order, cluster_map, leaf_sketch, level_sketch):
    place = jnp.stack([lax.axis_index(a) for a in ("z", "y", "core", "x")]).astype(jnp.int32)
    rows = row_order.shape[1]
    rank = leaf_sketch.shape[1]
    row_norm = float(lax.axis_size("x") * samples.shape[0])
    first, second, send_a, send_b, keep_a, keep_b = prepare(
        samples, row_order, cluster_map, leaf_sketch, place
    )

    def to_cluster(packed):
        packed = packed.reshape(-1, 2 * rows, rank)
        return lax.all_to_all(packed, ("z", "y"), split_axis=0, concat_axis=0, tiled=True)

    got_b = swap(send_b, "core", 1)
    send_a, got_b = lax.optimization_barrier((send_a, got_b))
    got_a = swap(send_a, "core", 1)
    second = swap(second, "core", 1)
    keep_a, got_a = (v.reshape(8, 2, 8, -1, v.shape[-1]) for v in (keep_a, got_a))
    keep_b, got_b = (v.reshape(8, 2, 8, -1, v.shape[-1]) for v in (keep_b, got_b))
    term_a = lambda i, n: keep_a[i : i + n] + got_a[i : i + n]
    term_b = lambda i, n: keep_b[i : i + n] + got_b[i : i + n]
    sends_b, first = lax.optimization_barrier((ring_sends(term_b), first))
    low_b, high_b, sends_a = ring_finish(term_b, sends_b, "y", ring_sends(term_a))
    low_a, high_a, _ = ring_finish(term_a, sends_a, "x")
    first = to_cluster(first)
    part_a = jnp.concatenate([low_a, high_a], axis=0).reshape(8, 4, -1, low_a.shape[-1])
    part_b = jnp.concatenate([low_b, high_b], axis=0).reshape(8, 4, -1, low_b.shape[-1])
    low_a, high_a = scatter_ring(lambda i, n: part_a[i : i + n], "y")
    low_b, high_b = scatter_ring(lambda i, n: part_b[i : i + n], "x")
    part_a = jnp.concatenate([low_a, high_a], axis=0)
    part_b = jnp.concatenate([low_b, high_b], axis=0)
    total = jnp.concatenate([part_a, part_b], axis=1)
    total = total.reshape(4, 2, *total.shape[1:])
    total = total[0] + swap(total[1], "z", 2) + swap(total[2], "z", 1) + swap(total[3], "z", 3)
    second, total, first = lax.optimization_barrier((second, total, first))
    total = total[0] + swap(total[1], "z", 4)
    second = to_cluster(second)
    chunks = (total,) + tuple(swap(total, "x", mask) for mask in (1, 2, 3))
    parts, node = leaf_node(place, chunks, leaf_sketch, row_norm)
    halves = []
    for depth, (axis, bit) in enumerate((("core", 1), ("y", 1), ("y", 2))):
        other = swap(node, axis, bit)
        if depth == 1:
            basis, other = lax.optimization_barrier((bases(place, first, parts, 0), other))
        last = depth == LEVELS - 1
        half, node = merge(node, other, level_sketch[depth], halves if last else ())
        halves.append(half)
    basis = bases(place, second, parts, 1, basis).reshape(-1, rank)
    return (basis, halves[-1][None], node[None])


def solution(mesh):
    grid = Mesh(mesh.devices.reshape(8, 4, 2, 4), ("z", "y", "core", "x"))
    every = ("z", "y", "core", "x")
    leaf = ("z", "y", "core")
    in_specs = (P(every, None), P(every, None), P(every), P(), P())
    out_specs = (P(every, None), P(leaf, None, None, None), P(leaf, None, None))
    return jax.shard_map(body, mesh=grid, in_specs=in_specs, out_specs=out_specs, check_vma=False)
```

```python
import functools
import math

import jax
import jax.numpy as jnp
from jax import lax
from jax.experimental import pallas as pl
from jax.experimental.pallas import tpu as pltpu
from jax.sharding import Mesh, PartitionSpec as P

LEVELS = 3
SHIFT = 0.01
PANEL = 32
HIGHEST = lax.Precision.HIGHEST
F32 = jnp.float32
BF16 = jnp.bfloat16
VMEM_LIMIT = 56 * 2**20

NT = (((1,), (1,)), ((), ()))
TN = (((0,), (0,)), ((), ()))


def exact(a, b, dims=(((1,), (0,)), ((), ()))):
    return lax.dot_general(a, b, dims, precision=HIGHEST, preferred_element_type=F32)


def cholesky_inverse(work, inverse):
    n = inverse.shape[0]
    row = lax.broadcasted_iota(jnp.int32, (PANEL, n), 0)
    for first in range(0, n, PANEL):
        left = work[first : first + PANEL, :n]
        right = work[first : first + PANEL, n:]
        cols = [
            jnp.broadcast_to(left[:, first + j : first + j + 1], (PANEL, n)) for j in range(PANEL)
        ]
        scale = jnp.zeros((PANEL, n), F32)
        for j in range(PANEL):
            pivot = cols[j][j : j + 1]
            factor = jnp.where(row > j, cols[j] * (1.0 / pivot), 0.0)
            scale = jnp.where(row == j, lax.rsqrt(pivot), scale)
            left = left - factor * left[j : j + 1]
            right = right - factor * right[j : j + 1]
            for k in range(j + 1, PANEL):
                cols[k] = cols[k] - factor * cols[k][j : j + 1]
        left = left * scale
        right = right * scale
        inverse[first : first + PANEL, :] = right
        rest = first + PANEL
        if rest < n:
            both = jnp.concatenate([left, right], axis=1)
            update = exact(left, both, TN)
            work[rest:, :] = work[rest:, :] - update[rest:, :]


def identity(n):
    shape = (n, n)
    return (
        lax.broadcasted_iota(jnp.int32, shape, 0) == lax.broadcasted_iota(jnp.int32, shape, 1)
    ).astype(F32)


def prep_kernel(
    map_ref, place_ref, order_ref, samples_hbm, sketch_ref,
    first_ref, second_ref, send_a, send_b, keep_a, keep_b,
    parts, ordered, slots, count, columns, samples_ref, arrived,
):
    blocks, rows, width = samples_ref.shape
    zs, ys, cores, xs = 8, 4, 2, 4
    rank = sketch_ref.shape[1]
    group = columns.shape[0]
    each = blocks // group
    step = pl.program_id(0)

    def load(g):
        some = pl.ds(g * each, each)
        return pltpu.make_async_copy(samples_hbm.at[some], samples_ref.at[some], arrived.at[g])

    @pl.when(step == 0)
    def _():
        for g in range(group):
            load(g).start()
        clusters = count.shape[0]

        def clear(c, _):
            count[c] = 0
            slots[2 * c] = blocks
            slots[2 * c + 1] = blocks
            return 0

        lax.fori_loop(0, clusters, clear, 0)

        def place(b, _):
            c = map_ref[b]
            slots[2 * c + count[c]] = b
            count[c] = count[c] + 1
            return 0

        lax.fori_loop(0, blocks, place, 0)
        parts[blocks] = jnp.zeros((2 * rank, rows), BF16)
        ordered[blocks] = jnp.zeros((rows, rank), BF16)
        turned = order_ref[...].astype(F32).T
        for g in range(group):
            columns[g] = turned[:, g * each : (g + 1) * each]
        sketch_t = sketch_ref[...].astype(F32).T.astype(BF16)
        lane = lax.broadcasted_iota(jnp.int32, (rows, rows), 1).astype(F32)

        def some(g, _):
            load(g).wait()
            column = columns[g]
            for u in range(each):
                b = g * each + u
                value = lax.dot_general(
                    sketch_t, samples_ref[b], NT, preferred_element_type=F32
                )
                high = value.astype(BF16)
                low = (value - high.astype(F32)).astype(BF16)
                parts[b, :rank, :] = high
                parts[b, rank:, :] = low
                pick = (jnp.broadcast_to(column[:, u : u + 1], (rows, rows)) == lane).astype(F32)
                ordered[b] = lax.dot_general(
                    pick.astype(BF16), high, NT, preferred_element_type=F32
                ).astype(BF16)
            return 0

        lax.fori_loop(0, group, some, 0)

    my_z, my_y, my_core, my_x = (place_ref[i] for i in range(4))
    y = lax.rem(my_y + step, ys)
    quarter = rows // 2 // xs

    def one(z_rel, _):
        flip = ((z_rel & 1) << 2) | (z_rel & 2) | (z_rel >> 2)
        z = my_z ^ flip
        for k_rel, out_a, out_b in ((0, keep_a, keep_b), (1, send_a, send_b)):
            core = my_core if k_rel == 0 else 1 - my_core
            cluster = (z * ys + y) * cores + core
            b0 = slots[2 * cluster]
            b1 = slots[2 * cluster + 1]
            out = first_ref if k_rel == 0 else second_ref
            out[z, 0, :rows] = ordered[b0]
            out[z, 0, rows:] = ordered[b1]
            lhs = jnp.concatenate([parts[b0], parts[b1]], axis=1)
            rhs = jnp.concatenate(
                [samples_ref[jnp.minimum(b0, blocks - 1)], samples_ref[jnp.minimum(b1, blocks - 1)]],
                axis=0,
            )
            both = jnp.dot(lhs, rhs, preferred_element_type=F32)
            total = both[:rank] + both[rank:]
            for x in range(xs):
                x_rel = lax.rem(x - my_x + xs, xs)
                out_a[x_rel, 0, 0, z_rel] = total[x * quarter : (x + 1) * quarter]
                out_b[0, x_rel, z_rel] = total[rank // 2 + x * quarter : rank // 2 + (x + 1) * quarter]
        return 0

    lax.fori_loop(0, zs, one, 0, unroll=8)


def prepare(samples, row_order, cluster_map, leaf_sketch, place):
    blocks, rows = row_order.shape
    width = samples.shape[1]
    rank = leaf_sketch.shape[1]
    samples = samples.reshape(blocks, rows, width)
    zs, ys, cores, xs = 8, 4, 2, 4
    quarter = rows // 2 // xs
    chunk_a = jax.ShapeDtypeStruct((xs, 2, ys // 2, zs, quarter, width), F32)
    chunk_b = jax.ShapeDtypeStruct((ys, xs, zs, quarter, width), F32)
    spec_a = pl.BlockSpec((xs, 1, 1, zs, quarter, width), lambda i, m, p: (0, i // 2, i % 2, 0, 0, 0))
    spec_b = pl.BlockSpec((1, xs, zs, quarter, width), lambda i, m, p: (i, 0, 0, 0, 0))
    packed = jax.ShapeDtypeStruct((zs, ys, 2 * rows, rank), BF16)
    packed_spec = pl.BlockSpec(
        (zs, 1, 2 * rows, rank), lambda i, m, p: (0, lax.rem(p[1] + i, 4), 0, 0)
    )
    return pl.pallas_call(
        prep_kernel,
        out_shape=(packed, packed, chunk_a, chunk_b, chunk_a, chunk_b),
        grid_spec=pltpu.PrefetchScalarGridSpec(
            num_scalar_prefetch=2,
            grid=(ys,),
            in_specs=[
                pl.BlockSpec(row_order.shape, lambda i, m, p: (0, 0)),
                pl.BlockSpec(memory_space=pl.ANY),
                pl.BlockSpec(leaf_sketch.shape, lambda i, m, p: (0, 0)),
            ],
            out_specs=[packed_spec, packed_spec, spec_a, spec_b, spec_a, spec_b],
            scratch_shapes=[
                pltpu.VMEM((blocks + 1, 2 * rank, rows), BF16),
                pltpu.VMEM((blocks + 1, rows, rank), BF16),
                pltpu.SMEM((2 * zs * ys * cores,), jnp.int32),
                pltpu.SMEM((zs * ys * cores,), jnp.int32),
                pltpu.VMEM((8, rows, blocks // 8), F32),
                pltpu.VMEM(samples.shape, BF16),
                pltpu.SemaphoreType.DMA((8,)),
            ],
        ),
        compiler_params=pltpu.CompilerParams(vmem_limit_bytes=VMEM_LIMIT),
        cost_estimate=pl.CostEstimate(
            flops=6 * 10**9, bytes_accessed=16 * 2**20, transcendentals=0
        ),
        name="prepare",
    )(cluster_map, place, row_order, samples, leaf_sketch)


def leaf_kernel(row_norm, place_ref, c0, c1, c2, c3, sketch_ref, parts_ref, node_ref, cross, work, inverse):
    rank, width = node_ref.shape
    quarter = rank // 8
    my_x = place_ref[3]
    for rel, chunk in enumerate((c0, c1, c2, c3)):
        start = pl.multiple_of((my_x ^ rel) * quarter, quarter)
        cross[pl.ds(start, quarter), :] = chunk[:quarter, :]
        cross[pl.ds(start + rank // 2, quarter), :] = chunk[quarter:, :]
    eye = identity(rank)
    gram = exact(cross[...], sketch_ref[...].astype(F32)) / row_norm + SHIFT * eye
    work[:, :rank] = gram
    work[:, rank:] = eye
    cholesky_inverse(work, inverse)
    whole = inverse[...]
    high = whole.astype(BF16)
    parts_ref[:, :rank] = high
    parts_ref[:, rank:] = (whole - high.astype(F32)).astype(BF16)
    node_ref[...] = exact(whole, cross[...]) * (math.sqrt(width) / row_norm)


def leaf_node(place, chunks, leaf_sketch, row_norm):
    rank = leaf_sketch.shape[1]
    width = leaf_sketch.shape[0]
    vmem = pl.BlockSpec(memory_space=pltpu.VMEM)
    return pl.pallas_call(
        functools.partial(leaf_kernel, row_norm),
        out_shape=(
            jax.ShapeDtypeStruct((rank, 2 * rank), BF16),
            jax.ShapeDtypeStruct((rank, width), F32),
        ),
        in_specs=[pl.BlockSpec(memory_space=pltpu.SMEM)] + [vmem] * 5,
        out_specs=(vmem, vmem),
        scratch_shapes=[
            pltpu.VMEM((rank, width), F32),
            pltpu.VMEM((rank, 2 * rank), F32),
            pltpu.VMEM((rank, rank), F32),
        ],
        compiler_params=pltpu.CompilerParams(vmem_limit_bytes=16 * 2**20),
        cost_estimate=pl.CostEstimate(flops=9*10**9, bytes_accessed=2**16, transcendentals=0),
        name="leaf_node",
    )(place, *chunks, leaf_sketch)


def merge_kernel(own_ref, other_ref, sketch_ref, *refs):
    *earlier, transfer_ref, node_ref, work, inverse = refs
    for i, half in enumerate(earlier):
        transfer_ref[i] = half[0]
    rank, width = node_ref.shape
    total = 2.0 * rank
    sketch = sketch_ref[...]
    own, other = own_ref[...], other_ref[...]
    own_z = exact(own, sketch)
    other_z = exact(other, sketch)
    z = jnp.concatenate([own_z, other_z], axis=0)
    stacked = jnp.concatenate([own, other], axis=0)
    z_t = z.T
    gram = exact(z_t, z) / total
    product = exact(z_t, stacked)
    eye = identity(rank)
    work[:, :rank] = gram + SHIFT * eye
    work[:, rank:] = eye
    cholesky_inverse(work, inverse)
    whole = inverse[...]
    node_ref[...] = exact(whole, product) * (math.sqrt(width) / total)
    transfer_ref[len(earlier)] = exact(own_z, whole, NT)


def merge(own, other, sketch, earlier=()):
    rank, width = own.shape
    vmem = pl.BlockSpec(memory_space=pltpu.VMEM)
    return pl.pallas_call(
        merge_kernel,
        out_shape=(
            jax.ShapeDtypeStruct((len(earlier) + 1, rank, rank), F32),
            jax.ShapeDtypeStruct((rank, width), F32),
        ),
        in_specs=[vmem] * (3 + len(earlier)),
        out_specs=(vmem, vmem),
        scratch_shapes=[pltpu.VMEM((rank, 2 * rank), F32), pltpu.VMEM((rank, rank), F32)],
        compiler_params=pltpu.CompilerParams(vmem_limit_bytes=16 * 2**20),
        cost_estimate=pl.CostEstimate(flops=9*10**9, bytes_accessed=2**16, transcendentals=0),
        name="merge",
    )(own, other, sketch, *earlier)


def bases_kernel(place_ref, rows_ref, parts_ref, *refs):
    out_ref = refs[-1]
    rows = rows_ref[...].reshape(-1, rows_ref.shape[-1])
    out_ref[...] = (
        lax.dot_general(
            jnp.concatenate([rows, rows], axis=1), parts_ref[...], NT, preferred_element_type=F32
        )
        .astype(BF16)
        .reshape(out_ref.shape)
    )


def bases(place, rows, parts, other, before=None):
    sources, height, rank = rows.shape
    tile = 16
    args = (place, rows, parts)
    in_specs = [
        pl.BlockSpec((tile, height, rank), lambda i, p: (i, 0, 0)),
        pl.BlockSpec(parts.shape, lambda i, p: (0, 0)),
    ]
    aliases = {}
    if before is not None:
        args += (before,)
        in_specs.append(pl.BlockSpec(memory_space=pl.ANY))
        aliases = {3: 0}
    total = sources * height
    return pl.pallas_call(
        bases_kernel,
        out_shape=jax.ShapeDtypeStruct((sources, 2, height, rank), BF16),
        grid_spec=pltpu.PrefetchScalarGridSpec(
            num_scalar_prefetch=1,
            grid=(sources // tile,),
            in_specs=in_specs,
            out_specs=pl.BlockSpec(
                (tile, 1, height, rank), lambda i, p: (i, p[2] ^ other, 0, 0)
            ),
        ),
        input_output_aliases=aliases,
        compiler_params=pltpu.CompilerParams(vmem_limit_bytes=32 * 2**20),
        cost_estimate=pl.CostEstimate(
            flops=4 * total * rank * rank, bytes_accessed=4 * total * rank, transcendentals=0
        ),
        name="bases",
    )(*args)


def shift(value, axis, distance):
    size = lax.axis_size(axis)
    return lax.ppermute(value, axis, [(i, (i + distance) % size) for i in range(size)])


def swap(value, axis, mask):
    return lax.ppermute(value, axis, [(i, i ^ mask) for i in range(lax.axis_size(axis))])


def ring_sends(term):
    return term(3, 2), term(5, 2)


def ring_lasts(term, got):
    return term(2, 1) + got[0][1:], term(7, 1) + got[1][:1]


def ring_sum(term, got, last):
    own = term(0, 2)
    return own[0] + got[1][1] + last[0][0], own[1] + got[0][0] + last[1][0]


def both_ways(sends, axis):
    return shift(sends[0], axis, 1), shift(sends[1], axis, -1)


def after(value, work):
    return lax.optimization_barrier((value, work))[0]


def scatter_ring(term, axis):
    got = both_ways(ring_sends(term), axis)
    return ring_sum(term, got, both_ways(ring_lasts(term, got), axis))


def body(samples, row_order, cluster_map, leaf_sketch, level_sketch):
    place = jnp.stack([lax.axis_index(a) for a in ("z", "y", "core", "x")]).astype(jnp.int32)
    rows = row_order.shape[1]
    rank = leaf_sketch.shape[1]
    row_norm = float(lax.axis_size("x") * samples.shape[0])
    first, second, send_a, send_b, keep_a, keep_b = prepare(
        samples, row_order, cluster_map, leaf_sketch, place
    )

    def to_cluster(packed):
        packed = packed.reshape(-1, 2 * rows, rank)
        return lax.all_to_all(packed, ("z", "y"), split_axis=0, concat_axis=0, tiled=True)

    got_b = swap(send_b, "core", 1)
    send_a, got_b = lax.optimization_barrier((send_a, got_b))
    got_a = swap(send_a, "core", 1)
    second = swap(second, "core", 1)
    keep_a, got_a = (v.reshape(8, 2, 8, -1, v.shape[-1]) for v in (keep_a, got_a))
    keep_b, got_b = (v.reshape(8, 2, 8, -1, v.shape[-1]) for v in (keep_b, got_b))
    term_a = lambda i, n: keep_a[i : i + n] + got_a[i : i + n]
    term_b = lambda i, n: keep_b[i : i + n] + got_b[i : i + n]
    sends_b, first = lax.optimization_barrier((ring_sends(term_b), first))
    sends_a = ring_sends(term_a)
    one_b = both_ways(sends_b, "y")
    one_a = both_ways(sends_a, "x")
    one_b = after(one_b, sends_a)
    two_b = both_ways(ring_lasts(term_b, one_b), "y")
    lasts_a = ring_lasts(term_a, one_a)
    two_a = both_ways(lasts_a, "x")
    low_b, high_b = ring_sum(term_b, one_b, after(two_b, lasts_a))
    low_a, high_a = ring_sum(term_a, one_a, two_a)
    first = to_cluster(first)
    part_a = jnp.concatenate([low_a, high_a], axis=0).reshape(8, 4, -1, low_a.shape[-1])
    part_b = jnp.concatenate([low_b, high_b], axis=0).reshape(8, 4, -1, low_b.shape[-1])
    low_a, high_a = scatter_ring(lambda i, n: part_a[i : i + n], "y")
    low_b, high_b = scatter_ring(lambda i, n: part_b[i : i + n], "x")
    part_a = jnp.concatenate([low_a, high_a], axis=0)
    part_b = jnp.concatenate([low_b, high_b], axis=0)
    total = jnp.concatenate([part_a, part_b], axis=1)
    total = total.reshape(4, 2, *total.shape[1:])
    total = total[0] + swap(total[1], "z", 2) + swap(total[2], "z", 1) + swap(total[3], "z", 3)
    second, total, first = lax.optimization_barrier((second, total, first))
    total = total[0] + swap(total[1], "z", 4)
    second = to_cluster(second)
    chunks = (total,) + tuple(swap(total, "x", mask) for mask in (1, 2, 3))
    parts, node = leaf_node(place, chunks, leaf_sketch, row_norm)
    halves = []
    for depth, (axis, bit) in enumerate((("core", 1), ("y", 1), ("y", 2))):
        other = swap(node, axis, bit)
        if depth == 1:
            basis, other = lax.optimization_barrier((bases(place, first, parts, 0), other))
        last = depth == LEVELS - 1
        half, node = merge(node, other, level_sketch[depth], halves if last else ())
        halves.append(half)
    basis = bases(place, second, parts, 1, basis).reshape(-1, rank)
    return (basis, halves[-1][None], node[None])


def solution(mesh):
    grid = Mesh(mesh.devices.reshape(8, 4, 2, 4), ("z", "y", "core", "x"))
    every = ("z", "y", "core", "x")
    leaf = ("z", "y", "core")
    in_specs = (P(every, None), P(every, None), P(every), P(), P())
    out_specs = (P(every, None), P(leaf, None, None, None), P(leaf, None, None))
    return jax.shard_map(body, mesh=grid, in_specs=in_specs, out_specs=out_specs, check_vma=False)
```

```python
import functools
import math

import jax
import jax.numpy as jnp
from jax import lax
from jax.experimental import pallas as pl
from jax.experimental.pallas import tpu as pltpu
from jax.sharding import Mesh, PartitionSpec as P

LEVELS = 3
SHIFT = 0.01
SPLIT = 24
PANEL = 32
HIGHEST = lax.Precision.HIGHEST
F32 = jnp.float32
BF16 = jnp.bfloat16
VMEM_LIMIT = 56 * 2**20

NT = (((1,), (1,)), ((), ()))
TN = (((0,), (0,)), ((), ()))


def exact(a, b, dims=(((1,), (0,)), ((), ()))):
    return lax.dot_general(a, b, dims, precision=HIGHEST, preferred_element_type=F32)


def cholesky_inverse(work, inverse):
    n = inverse.shape[0]
    row = lax.broadcasted_iota(jnp.int32, (PANEL, n), 0)
    for first in range(0, n, PANEL):
        left = work[first : first + PANEL, :n]
        right = work[first : first + PANEL, n:]
        cols = [
            jnp.broadcast_to(left[:, first + j : first + j + 1], (PANEL, n)) for j in range(PANEL)
        ]
        scale = jnp.zeros((PANEL, n), F32)
        for j in range(PANEL):
            pivot = cols[j][j : j + 1]
            factor = jnp.where(row > j, cols[j] * (1.0 / pivot), 0.0)
            scale = jnp.where(row == j, lax.rsqrt(pivot), scale)
            left = left - factor * left[j : j + 1]
            right = right - factor * right[j : j + 1]
            for k in range(j + 1, PANEL):
                cols[k] = cols[k] - factor * cols[k][j : j + 1]
        left = left * scale
        right = right * scale
        inverse[first : first + PANEL, :] = right
        rest = first + PANEL
        if rest < n:
            both = jnp.concatenate([left, right], axis=1)
            update = exact(left, both, TN)
            work[rest:, :] = work[rest:, :] - update[rest:, :]


def identity(n):
    shape = (n, n)
    return (
        lax.broadcasted_iota(jnp.int32, shape, 0) == lax.broadcasted_iota(jnp.int32, shape, 1)
    ).astype(F32)


def prep_kernel(
    map_ref, place_ref, order_ref, samples_hbm, sketch_ref,
    first_ref, second_ref, send_a, send_b, keep_a, keep_b,
    parts, ordered, slots, count, columns, samples_ref, arrived,
):
    blocks, rows, width = samples_ref.shape
    zs, ys, cores, xs = 8, 4, 2, 4
    rank = sketch_ref.shape[1]
    group = columns.shape[0]
    each = blocks // group
    step = pl.program_id(0)

    def load(g):
        some = pl.ds(g * each, each)
        return pltpu.make_async_copy(samples_hbm.at[some], samples_ref.at[some], arrived.at[g])

    @pl.when(step == 0)
    def _():
        for g in range(group):
            load(g).start()
        clusters = count.shape[0]

        def clear(c, _):
            count[c] = 0
            slots[2 * c] = blocks
            slots[2 * c + 1] = blocks
            return 0

        lax.fori_loop(0, clusters, clear, 0)

        def place(b, _):
            c = map_ref[b]
            slots[2 * c + count[c]] = b
            count[c] = count[c] + 1
            return 0

        lax.fori_loop(0, blocks, place, 0)
        parts[blocks] = jnp.zeros((2 * rank, rows), BF16)
        ordered[blocks] = jnp.zeros((rows, rank), BF16)
        turned = order_ref[...].astype(F32).T
        for g in range(group):
            columns[g] = turned[:, g * each : (g + 1) * each]
        sketch_t = sketch_ref[...].astype(F32).T.astype(BF16)
        lane = lax.broadcasted_iota(jnp.int32, (rows, rows), 1).astype(F32)

        def some(g, _):
            load(g).wait()
            column = columns[g]
            for u in range(each):
                b = g * each + u
                value = lax.dot_general(
                    sketch_t, samples_ref[b], NT, preferred_element_type=F32
                )
                high = value.astype(BF16)
                low = (value - high.astype(F32)).astype(BF16)
                parts[b, :rank, :] = high
                parts[b, rank:, :] = low
                pick = (jnp.broadcast_to(column[:, u : u + 1], (rows, rows)) == lane).astype(F32)
                ordered[b] = lax.dot_general(
                    pick.astype(BF16), high, NT, preferred_element_type=F32
                ).astype(BF16)
            return 0

        lax.fori_loop(0, group, some, 0)

    my_z, my_y, my_core, my_x = (place_ref[i] for i in range(4))
    y = lax.rem(my_y + step, ys)
    quarter = rank // xs

    def one(z_rel, _):
        flip = ((z_rel & 1) << 2) | (z_rel & 2) | (z_rel >> 2)
        z = my_z ^ flip
        for k_rel, out_a, out_b in ((0, keep_a, keep_b), (1, send_a, send_b)):
            core = my_core if k_rel == 0 else 1 - my_core
            cluster = (z * ys + y) * cores + core
            b0 = slots[2 * cluster]
            b1 = slots[2 * cluster + 1]
            out = first_ref if k_rel == 0 else second_ref
            out[z, 0, :rows] = ordered[b0]
            out[z, 0, rows:] = ordered[b1]
            lhs = jnp.concatenate([parts[b0], parts[b1]], axis=1)
            rhs = jnp.concatenate(
                [samples_ref[jnp.minimum(b0, blocks - 1)], samples_ref[jnp.minimum(b1, blocks - 1)]],
                axis=0,
            )
            both = jnp.dot(lhs, rhs, preferred_element_type=F32)
            total = both[:rank] + both[rank:]
            for x in range(xs):
                x_rel = lax.rem(x - my_x + xs, xs)
                top = x * quarter
                out_a[x_rel, 0, 0, z_rel] = total[top : top + SPLIT]
                out_b[0, x_rel, z_rel] = total[top + SPLIT : top + quarter]
        return 0

    lax.fori_loop(0, zs, one, 0, unroll=8)


def prepare(samples, row_order, cluster_map, leaf_sketch, place):
    blocks, rows = row_order.shape
    width = samples.shape[1]
    rank = leaf_sketch.shape[1]
    samples = samples.reshape(blocks, rows, width)
    zs, ys, cores, xs = 8, 4, 2, 4
    rest = rank // xs - SPLIT
    chunk_a = jax.ShapeDtypeStruct((xs, 2, ys // 2, zs, SPLIT, width), F32)
    chunk_b = jax.ShapeDtypeStruct((ys, xs, zs, rest, width), F32)
    spec_a = pl.BlockSpec((xs, 1, 1, zs, SPLIT, width), lambda i, m, p: (0, i // 2, i % 2, 0, 0, 0))
    spec_b = pl.BlockSpec((1, xs, zs, rest, width), lambda i, m, p: (i, 0, 0, 0, 0))
    packed = jax.ShapeDtypeStruct((zs, ys, 2 * rows, rank), BF16)
    packed_spec = pl.BlockSpec(
        (zs, 1, 2 * rows, rank), lambda i, m, p: (0, lax.rem(p[1] + i, 4), 0, 0)
    )
    return pl.pallas_call(
        prep_kernel,
        out_shape=(packed, packed, chunk_a, chunk_b, chunk_a, chunk_b),
        grid_spec=pltpu.PrefetchScalarGridSpec(
            num_scalar_prefetch=2,
            grid=(ys,),
            in_specs=[
                pl.BlockSpec(row_order.shape, lambda i, m, p: (0, 0)),
                pl.BlockSpec(memory_space=pl.ANY),
                pl.BlockSpec(leaf_sketch.shape, lambda i, m, p: (0, 0)),
            ],
            out_specs=[packed_spec, packed_spec, spec_a, spec_b, spec_a, spec_b],
            scratch_shapes=[
                pltpu.VMEM((blocks + 1, 2 * rank, rows), BF16),
                pltpu.VMEM((blocks + 1, rows, rank), BF16),
                pltpu.SMEM((2 * zs * ys * cores,), jnp.int32),
                pltpu.SMEM((zs * ys * cores,), jnp.int32),
                pltpu.VMEM((8, rows, blocks // 8), F32),
                pltpu.VMEM(samples.shape, BF16),
                pltpu.SemaphoreType.DMA((8,)),
            ],
        ),
        compiler_params=pltpu.CompilerParams(vmem_limit_bytes=VMEM_LIMIT),
        cost_estimate=pl.CostEstimate(
            flops=6 * 10**9, bytes_accessed=16 * 2**20, transcendentals=0
        ),
        name="prepare",
    )(cluster_map, place, row_order, samples, leaf_sketch)


def leaf_kernel(row_norm, place_ref, c0, c1, c2, c3, sketch_ref, parts_ref, node_ref, cross, work, inverse):
    rank, width = node_ref.shape
    quarter = rank // 4
    my_x = place_ref[3]
    for rel, chunk in enumerate((c0, c1, c2, c3)):
        start = pl.multiple_of((my_x ^ rel) * quarter, quarter)
        cross[pl.ds(start, quarter), :] = chunk[...]
    eye = identity(rank)
    gram = exact(cross[...], sketch_ref[...].astype(F32)) / row_norm + SHIFT * eye
    work[:, :rank] = gram
    work[:, rank:] = eye
    cholesky_inverse(work, inverse)
    whole = inverse[...]
    high = whole.astype(BF16)
    parts_ref[:, :rank] = high
    parts_ref[:, rank:] = (whole - high.astype(F32)).astype(BF16)
    node_ref[...] = exact(whole, cross[...]) * (math.sqrt(width) / row_norm)


def leaf_node(place, chunks, leaf_sketch, row_norm):
    rank = leaf_sketch.shape[1]
    width = leaf_sketch.shape[0]
    vmem = pl.BlockSpec(memory_space=pltpu.VMEM)
    return pl.pallas_call(
        functools.partial(leaf_kernel, row_norm),
        out_shape=(
            jax.ShapeDtypeStruct((rank, 2 * rank), BF16),
            jax.ShapeDtypeStruct((rank, width), F32),
        ),
        in_specs=[pl.BlockSpec(memory_space=pltpu.SMEM)] + [vmem] * 5,
        out_specs=(vmem, vmem),
        scratch_shapes=[
            pltpu.VMEM((rank, width), F32),
            pltpu.VMEM((rank, 2 * rank), F32),
            pltpu.VMEM((rank, rank), F32),
        ],
        compiler_params=pltpu.CompilerParams(vmem_limit_bytes=16 * 2**20),
        cost_estimate=pl.CostEstimate(flops=9*10**9, bytes_accessed=2**16, transcendentals=0),
        name="leaf_node",
    )(place, *chunks, leaf_sketch)


def merge_kernel(own_ref, other_ref, sketch_ref, *refs):
    *earlier, transfer_ref, node_ref, work, inverse = refs
    for i, half in enumerate(earlier):
        transfer_ref[i] = half[0]
    rank, width = node_ref.shape
    total = 2.0 * rank
    sketch = sketch_ref[...]
    own, other = own_ref[...], other_ref[...]
    own_z = exact(own, sketch)
    other_z = exact(other, sketch)
    z = jnp.concatenate([own_z, other_z], axis=0)
    stacked = jnp.concatenate([own, other], axis=0)
    z_t = z.T
    gram = exact(z_t, z) / total
    product = exact(z_t, stacked)
    eye = identity(rank)
    work[:, :rank] = gram + SHIFT * eye
    work[:, rank:] = eye
    cholesky_inverse(work, inverse)
    whole = inverse[...]
    node_ref[...] = exact(whole, product) * (math.sqrt(width) / total)
    transfer_ref[len(earlier)] = exact(own_z, whole, NT)


def merge(own, other, sketch, earlier=()):
    rank, width = own.shape
    vmem = pl.BlockSpec(memory_space=pltpu.VMEM)
    return pl.pallas_call(
        merge_kernel,
        out_shape=(
            jax.ShapeDtypeStruct((len(earlier) + 1, rank, rank), F32),
            jax.ShapeDtypeStruct((rank, width), F32),
        ),
        in_specs=[vmem] * (3 + len(earlier)),
        out_specs=(vmem, vmem),
        scratch_shapes=[pltpu.VMEM((rank, 2 * rank), F32), pltpu.VMEM((rank, rank), F32)],
        compiler_params=pltpu.CompilerParams(vmem_limit_bytes=16 * 2**20),
        cost_estimate=pl.CostEstimate(flops=9*10**9, bytes_accessed=2**16, transcendentals=0),
        name="merge",
    )(own, other, sketch, *earlier)


def bases_kernel(place_ref, rows_ref, parts_ref, *refs):
    out_ref = refs[-1]
    rows = rows_ref[...].reshape(-1, rows_ref.shape[-1])
    out_ref[...] = (
        lax.dot_general(
            jnp.concatenate([rows, rows], axis=1), parts_ref[...], NT, preferred_element_type=F32
        )
        .astype(BF16)
        .reshape(out_ref.shape)
    )


def bases(place, rows, parts, other, before=None):
    sources, height, rank = rows.shape
    tile = 16
    args = (place, rows, parts)
    in_specs = [
        pl.BlockSpec((tile, height, rank), lambda i, p: (i, 0, 0)),
        pl.BlockSpec(parts.shape, lambda i, p: (0, 0)),
    ]
    aliases = {}
    if before is not None:
        args += (before,)
        in_specs.append(pl.BlockSpec(memory_space=pl.ANY))
        aliases = {3: 0}
    total = sources * height
    return pl.pallas_call(
        bases_kernel,
        out_shape=jax.ShapeDtypeStruct((sources, 2, height, rank), BF16),
        grid_spec=pltpu.PrefetchScalarGridSpec(
            num_scalar_prefetch=1,
            grid=(sources // tile,),
            in_specs=in_specs,
            out_specs=pl.BlockSpec(
                (tile, 1, height, rank), lambda i, p: (i, p[2] ^ other, 0, 0)
            ),
        ),
        input_output_aliases=aliases,
        compiler_params=pltpu.CompilerParams(vmem_limit_bytes=32 * 2**20),
        cost_estimate=pl.CostEstimate(
            flops=4 * total * rank * rank, bytes_accessed=4 * total * rank, transcendentals=0
        ),
        name="bases",
    )(*args)


def shift(value, axis, distance):
    size = lax.axis_size(axis)
    return lax.ppermute(value, axis, [(i, (i + distance) % size) for i in range(size)])


def swap(value, axis, mask):
    return lax.ppermute(value, axis, [(i, i ^ mask) for i in range(lax.axis_size(axis))])


def ring_sends(term):
    return term(3, 2), term(5, 2)


def ring_lasts(term, got):
    return term(2, 1) + got[0][1:], term(7, 1) + got[1][:1]


def ring_sum(term, got, last):
    own = term(0, 2)
    return own[0] + got[1][1] + last[0][0], own[1] + got[0][0] + last[1][0]


def both_ways(sends, axis):
    return shift(sends[0], axis, 1), shift(sends[1], axis, -1)


def after(value, work):
    return lax.optimization_barrier((value, work))[0]


def scatter_ring(term, axis):
    got = both_ways(ring_sends(term), axis)
    return ring_sum(term, got, both_ways(ring_lasts(term, got), axis))


def body(samples, row_order, cluster_map, leaf_sketch, level_sketch):
    place = jnp.stack([lax.axis_index(a) for a in ("z", "y", "core", "x")]).astype(jnp.int32)
    rows = row_order.shape[1]
    rank = leaf_sketch.shape[1]
    row_norm = float(lax.axis_size("x") * samples.shape[0])
    first, second, send_a, send_b, keep_a, keep_b = prepare(
        samples, row_order, cluster_map, leaf_sketch, place
    )

    def to_cluster(packed):
        packed = packed.reshape(-1, 2 * rows, rank)
        return lax.all_to_all(packed, ("z", "y"), split_axis=0, concat_axis=0, tiled=True)

    got_a = swap(send_a, "core", 1)
    send_b, got_a = lax.optimization_barrier((send_b, got_a))
    got_b = swap(send_b, "core", 1)
    second = swap(second, "core", 1)
    keep_a, got_a = (v.reshape(8, 2, 8, -1, v.shape[-1]) for v in (keep_a, got_a))
    keep_b, got_b = (v.reshape(8, 2, 8, -1, v.shape[-1]) for v in (keep_b, got_b))
    term_a = lambda i, n: keep_a[i : i + n] + got_a[i : i + n]
    term_b = lambda i, n: keep_b[i : i + n] + got_b[i : i + n]
    sends_a, first = lax.optimization_barrier((ring_sends(term_a), first))
    sends_b = ring_sends(term_b)
    one_a = both_ways(sends_a, "x")
    one_b = both_ways(sends_b, "y")
    one_a = after(one_a, sends_b)
    two_a = both_ways(ring_lasts(term_a, one_a), "x")
    two_b = both_ways(ring_lasts(term_b, one_b), "y")
    low_a, high_a = ring_sum(term_a, one_a, two_a)
    low_b, high_b = ring_sum(term_b, one_b, two_b)
    first = to_cluster(first)
    part_a = jnp.concatenate([low_a, high_a], axis=0).reshape(8, 4, -1, low_a.shape[-1])
    part_b = jnp.concatenate([low_b, high_b], axis=0).reshape(8, 4, -1, low_b.shape[-1])
    low_a, high_a = scatter_ring(lambda i, n: part_a[i : i + n], "y")
    low_b, high_b = scatter_ring(lambda i, n: part_b[i : i + n], "x")
    part_a = jnp.concatenate([low_a, high_a], axis=0)
    part_b = jnp.concatenate([low_b, high_b], axis=0)
    total = jnp.concatenate([part_a, part_b], axis=1)
    total = total.reshape(4, 2, *total.shape[1:])
    total = total[0] + swap(total[1], "z", 2) + swap(total[2], "z", 1) + swap(total[3], "z", 3)
    second, total, first = lax.optimization_barrier((second, total, first))
    total = total[0] + swap(total[1], "z", 4)
    second = to_cluster(second)
    chunks = (total,) + tuple(swap(total, "x", mask) for mask in (1, 2, 3))
    parts, node = leaf_node(place, chunks, leaf_sketch, row_norm)
    halves = []
    for depth, (axis, bit) in enumerate((("core", 1), ("y", 1), ("y", 2))):
        other = swap(node, axis, bit)
        if depth == 1:
            basis, other = lax.optimization_barrier((bases(place, first, parts, 0), other))
        last = depth == LEVELS - 1
        half, node = merge(node, other, level_sketch[depth], halves if last else ())
        halves.append(half)
    basis = bases(place, second, parts, 1, basis).reshape(-1, rank)
    return (basis, halves[-1][None], node[None])


def solution(mesh):
    grid = Mesh(mesh.devices.reshape(8, 4, 2, 4), ("z", "y", "core", "x"))
    every = ("z", "y", "core", "x")
    leaf = ("z", "y", "core")
    in_specs = (P(every, None), P(every, None), P(every), P(), P())
    out_specs = (P(every, None), P(leaf, None, None, None), P(leaf, None, None))
    return jax.shard_map(body, mesh=grid, in_specs=in_specs, out_specs=out_specs, check_vma=False)
```

```python
import functools
import math

import jax
import jax.numpy as jnp
from jax import lax
from jax.experimental import pallas as pl
from jax.experimental.pallas import tpu as pltpu
from jax.sharding import Mesh, PartitionSpec as P

LEVELS = 3
SHIFT = 0.01
SPLIT = 16
PANEL = 32
HIGHEST = lax.Precision.HIGHEST
F32 = jnp.float32
BF16 = jnp.bfloat16
VMEM_LIMIT = 56 * 2**20

NT = (((1,), (1,)), ((), ()))
TN = (((0,), (0,)), ((), ()))


def exact(a, b, dims=(((1,), (0,)), ((), ()))):
    return lax.dot_general(a, b, dims, precision=HIGHEST, preferred_element_type=F32)


def cholesky_inverse(work, inverse):
    n = inverse.shape[0]
    row = lax.broadcasted_iota(jnp.int32, (PANEL, n), 0)
    for first in range(0, n, PANEL):
        left = work[first : first + PANEL, :n]
        right = work[first : first + PANEL, n:]
        cols = [
            jnp.broadcast_to(left[:, first + j : first + j + 1], (PANEL, n)) for j in range(PANEL)
        ]
        scale = jnp.zeros((PANEL, n), F32)
        for j in range(PANEL):
            pivot = cols[j][j : j + 1]
            factor = jnp.where(row > j, cols[j] * (1.0 / pivot), 0.0)
            scale = jnp.where(row == j, lax.rsqrt(pivot), scale)
            left = left - factor * left[j : j + 1]
            right = right - factor * right[j : j + 1]
            for k in range(j + 1, PANEL):
                cols[k] = cols[k] - factor * cols[k][j : j + 1]
        left = left * scale
        right = right * scale
        inverse[first : first + PANEL, :] = right
        rest = first + PANEL
        if rest < n:
            both = jnp.concatenate([left, right], axis=1)
            update = exact(left, both, TN)
            work[rest:, :] = work[rest:, :] - update[rest:, :]


def identity(n):
    shape = (n, n)
    return (
        lax.broadcasted_iota(jnp.int32, shape, 0) == lax.broadcasted_iota(jnp.int32, shape, 1)
    ).astype(F32)


def prep_kernel(
    map_ref, place_ref, order_ref, samples_hbm, sketch_ref,
    first_ref, second_ref, send_a, send_b, keep_a, keep_b,
    parts, ordered, slots, count, columns, samples_ref, arrived,
):
    blocks, rows, width = samples_ref.shape
    zs, ys, cores, xs = 8, 4, 2, 4
    rank = sketch_ref.shape[1]
    group = columns.shape[0]
    each = blocks // group
    step = pl.program_id(0)

    def load(g):
        some = pl.ds(g * each, each)
        return pltpu.make_async_copy(samples_hbm.at[some], samples_ref.at[some], arrived.at[g])

    @pl.when(step == 0)
    def _():
        for g in range(group):
            load(g).start()
        clusters = count.shape[0]

        def clear(c, _):
            count[c] = 0
            slots[2 * c] = blocks
            slots[2 * c + 1] = blocks
            return 0

        lax.fori_loop(0, clusters, clear, 0)

        def place(b, _):
            c = map_ref[b]
            slots[2 * c + count[c]] = b
            count[c] = count[c] + 1
            return 0

        lax.fori_loop(0, blocks, place, 0)
        parts[blocks] = jnp.zeros((2 * rank, rows), BF16)
        ordered[blocks] = jnp.zeros((rows, rank), BF16)
        turned = order_ref[...].astype(F32).T
        for g in range(group):
            columns[g] = turned[:, g * each : (g + 1) * each]
        sketch_t = sketch_ref[...].astype(F32).T.astype(BF16)
        lane = lax.broadcasted_iota(jnp.int32, (rows, rows), 1).astype(F32)

        def some(g, _):
            load(g).wait()
            column = columns[g]
            for u in range(each):
                b = g * each + u
                value = lax.dot_general(
                    sketch_t, samples_ref[b], NT, preferred_element_type=F32
                )
                high = value.astype(BF16)
                low = (value - high.astype(F32)).astype(BF16)
                parts[b, :rank, :] = high
                parts[b, rank:, :] = low
                pick = (jnp.broadcast_to(column[:, u : u + 1], (rows, rows)) == lane).astype(F32)
                ordered[b] = lax.dot_general(
                    pick.astype(BF16), high, NT, preferred_element_type=F32
                ).astype(BF16)
            return 0

        lax.fori_loop(0, group, some, 0)

    my_z, my_y, my_core, my_x = (place_ref[i] for i in range(4))
    y = lax.rem(my_y + step, ys)
    quarter = rank // xs

    def one(z_rel, _):
        flip = ((z_rel & 1) << 2) | (z_rel & 2) | (z_rel >> 2)
        z = my_z ^ flip
        for k_rel, out_a, out_b in ((0, keep_a, keep_b), (1, send_a, send_b)):
            core = my_core if k_rel == 0 else 1 - my_core
            cluster = (z * ys + y) * cores + core
            b0 = slots[2 * cluster]
            b1 = slots[2 * cluster + 1]
            out = first_ref if k_rel == 0 else second_ref
            out[z, 0, :rows] = ordered[b0]
            out[z, 0, rows:] = ordered[b1]
            lhs = jnp.concatenate([parts[b0], parts[b1]], axis=1)
            rhs = jnp.concatenate(
                [samples_ref[jnp.minimum(b0, blocks - 1)], samples_ref[jnp.minimum(b1, blocks - 1)]],
                axis=0,
            )
            both = jnp.dot(lhs, rhs, preferred_element_type=F32)
            total = both[:rank] + both[rank:]
            for x in range(xs):
                x_rel = lax.rem(x - my_x + xs, xs)
                top = x * quarter
                out_a[x_rel, 0, 0, z_rel] = total[top : top + SPLIT]
                out_b[0, x_rel, z_rel] = total[top + SPLIT : top + quarter]
        return 0

    lax.fori_loop(0, zs, one, 0, unroll=8)


def prepare(samples, row_order, cluster_map, leaf_sketch, place):
    blocks, rows = row_order.shape
    width = samples.shape[1]
    rank = leaf_sketch.shape[1]
    samples = samples.reshape(blocks, rows, width)
    zs, ys, cores, xs = 8, 4, 2, 4
    rest = rank // xs - SPLIT
    chunk_a = jax.ShapeDtypeStruct((xs, 2, ys // 2, zs, SPLIT, width), F32)
    chunk_b = jax.ShapeDtypeStruct((ys, xs, zs, rest, width), F32)
    spec_a = pl.BlockSpec((xs, 1, 1, zs, SPLIT, width), lambda i, m, p: (0, i // 2, i % 2, 0, 0, 0))
    spec_b = pl.BlockSpec((1, xs, zs, rest, width), lambda i, m, p: (i, 0, 0, 0, 0))
    packed = jax.ShapeDtypeStruct((zs, ys, 2 * rows, rank), BF16)
    packed_spec = pl.BlockSpec(
        (zs, 1, 2 * rows, rank), lambda i, m, p: (0, lax.rem(p[1] + i, 4), 0, 0)
    )
    return pl.pallas_call(
        prep_kernel,
        out_shape=(packed, packed, chunk_a, chunk_b, chunk_a, chunk_b),
        grid_spec=pltpu.PrefetchScalarGridSpec(
            num_scalar_prefetch=2,
            grid=(ys,),
            in_specs=[
                pl.BlockSpec(row_order.shape, lambda i, m, p: (0, 0)),
                pl.BlockSpec(memory_space=pl.ANY),
                pl.BlockSpec(leaf_sketch.shape, lambda i, m, p: (0, 0)),
            ],
            out_specs=[packed_spec, packed_spec, spec_a, spec_b, spec_a, spec_b],
            scratch_shapes=[
                pltpu.VMEM((blocks + 1, 2 * rank, rows), BF16),
                pltpu.VMEM((blocks + 1, rows, rank), BF16),
                pltpu.SMEM((2 * zs * ys * cores,), jnp.int32),
                pltpu.SMEM((zs * ys * cores,), jnp.int32),
                pltpu.VMEM((8, rows, blocks // 8), F32),
                pltpu.VMEM(samples.shape, BF16),
                pltpu.SemaphoreType.DMA((8,)),
            ],
        ),
        compiler_params=pltpu.CompilerParams(vmem_limit_bytes=VMEM_LIMIT),
        cost_estimate=pl.CostEstimate(
            flops=6 * 10**9, bytes_accessed=16 * 2**20, transcendentals=0
        ),
        name="prepare",
    )(cluster_map, place, row_order, samples, leaf_sketch)


def leaf_kernel(row_norm, place_ref, c0, c1, c2, c3, sketch_ref, parts_ref, node_ref, cross, work, inverse):
    rank, width = node_ref.shape
    quarter = rank // 4
    my_x = place_ref[3]
    for rel, chunk in enumerate((c0, c1, c2, c3)):
        start = pl.multiple_of((my_x ^ rel) * quarter, quarter)
        cross[pl.ds(start, quarter), :] = chunk[...]
    eye = identity(rank)
    gram = exact(cross[...], sketch_ref[...].astype(F32)) / row_norm + SHIFT * eye
    work[:, :rank] = gram
    work[:, rank:] = eye
    cholesky_inverse(work, inverse)
    whole = inverse[...]
    high = whole.astype(BF16)
    parts_ref[:, :rank] = high
    parts_ref[:, rank:] = (whole - high.astype(F32)).astype(BF16)
    node_ref[...] = exact(whole, cross[...]) * (math.sqrt(width) / row_norm)


def leaf_node(place, chunks, leaf_sketch, row_norm):
    rank = leaf_sketch.shape[1]
    width = leaf_sketch.shape[0]
    vmem = pl.BlockSpec(memory_space=pltpu.VMEM)
    return pl.pallas_call(
        functools.partial(leaf_kernel, row_norm),
        out_shape=(
            jax.ShapeDtypeStruct((rank, 2 * rank), BF16),
            jax.ShapeDtypeStruct((rank, width), F32),
        ),
        in_specs=[pl.BlockSpec(memory_space=pltpu.SMEM)] + [vmem] * 5,
        out_specs=(vmem, vmem),
        scratch_shapes=[
            pltpu.VMEM((rank, width), F32),
            pltpu.VMEM((rank, 2 * rank), F32),
            pltpu.VMEM((rank, rank), F32),
        ],
        compiler_params=pltpu.CompilerParams(vmem_limit_bytes=16 * 2**20),
        cost_estimate=pl.CostEstimate(flops=9*10**9, bytes_accessed=2**16, transcendentals=0),
        name="leaf_node",
    )(place, *chunks, leaf_sketch)


def merge_kernel(own_ref, other_ref, sketch_ref, *refs):
    *earlier, transfer_ref, node_ref, work, inverse = refs
    for i, half in enumerate(earlier):
        transfer_ref[i] = half[0]
    rank, width = node_ref.shape
    total = 2.0 * rank
    sketch = sketch_ref[...]
    own, other = own_ref[...], other_ref[...]
    own_z = exact(own, sketch)
    other_z = exact(other, sketch)
    z = jnp.concatenate([own_z, other_z], axis=0)
    stacked = jnp.concatenate([own, other], axis=0)
    z_t = z.T
    gram = exact(z_t, z) / total
    product = exact(z_t, stacked)
    eye = identity(rank)
    work[:, :rank] = gram + SHIFT * eye
    work[:, rank:] = eye
    cholesky_inverse(work, inverse)
    whole = inverse[...]
    node_ref[...] = exact(whole, product) * (math.sqrt(width) / total)
    transfer_ref[len(earlier)] = exact(own_z, whole, NT)


def merge(own, other, sketch, earlier=()):
    rank, width = own.shape
    vmem = pl.BlockSpec(memory_space=pltpu.VMEM)
    return pl.pallas_call(
        merge_kernel,
        out_shape=(
            jax.ShapeDtypeStruct((len(earlier) + 1, rank, rank), F32),
            jax.ShapeDtypeStruct((rank, width), F32),
        ),
        in_specs=[vmem] * (3 + len(earlier)),
        out_specs=(vmem, vmem),
        scratch_shapes=[pltpu.VMEM((rank, 2 * rank), F32), pltpu.VMEM((rank, rank), F32)],
        compiler_params=pltpu.CompilerParams(vmem_limit_bytes=16 * 2**20),
        cost_estimate=pl.CostEstimate(flops=9*10**9, bytes_accessed=2**16, transcendentals=0),
        name="merge",
    )(own, other, sketch, *earlier)


def bases_kernel(place_ref, rows_ref, parts_ref, *refs):
    out_ref = refs[-1]
    rows = rows_ref[...].reshape(-1, rows_ref.shape[-1])
    out_ref[...] = (
        lax.dot_general(
            jnp.concatenate([rows, rows], axis=1), parts_ref[...], NT, preferred_element_type=F32
        )
        .astype(BF16)
        .reshape(out_ref.shape)
    )


def bases(place, rows, parts, other, before=None):
    sources, height, rank = rows.shape
    tile = 16
    args = (place, rows, parts)
    in_specs = [
        pl.BlockSpec((tile, height, rank), lambda i, p: (i, 0, 0)),
        pl.BlockSpec(parts.shape, lambda i, p: (0, 0)),
    ]
    aliases = {}
    if before is not None:
        args += (before,)
        in_specs.append(pl.BlockSpec(memory_space=pl.ANY))
        aliases = {3: 0}
    total = sources * height
    return pl.pallas_call(
        bases_kernel,
        out_shape=jax.ShapeDtypeStruct((sources, 2, height, rank), BF16),
        grid_spec=pltpu.PrefetchScalarGridSpec(
            num_scalar_prefetch=1,
            grid=(sources // tile,),
            in_specs=in_specs,
            out_specs=pl.BlockSpec(
                (tile, 1, height, rank), lambda i, p: (i, p[2] ^ other, 0, 0)
            ),
        ),
        input_output_aliases=aliases,
        compiler_params=pltpu.CompilerParams(vmem_limit_bytes=32 * 2**20),
        cost_estimate=pl.CostEstimate(
            flops=4 * total * rank * rank, bytes_accessed=4 * total * rank, transcendentals=0
        ),
        name="bases",
    )(*args)


def shift(value, axis, distance):
    size = lax.axis_size(axis)
    return lax.ppermute(value, axis, [(i, (i + distance) % size) for i in range(size)])


def swap(value, axis, mask):
    return lax.ppermute(value, axis, [(i, i ^ mask) for i in range(lax.axis_size(axis))])


def ring_sends(term):
    return term(3, 2), term(5, 2)


def ring_lasts(term, got):
    return term(2, 1) + got[0][1:], term(7, 1) + got[1][:1]


def ring_sum(term, got, last):
    own = term(0, 2)
    return own[0] + got[1][1] + last[0][0], own[1] + got[0][0] + last[1][0]


def both_ways(sends, axis):
    return shift(sends[0], axis, 1), shift(sends[1], axis, -1)


def after(value, work):
    return lax.optimization_barrier((value, work))[0]


def scatter_ring(term, axis):
    got = both_ways(ring_sends(term), axis)
    return ring_sum(term, got, both_ways(ring_lasts(term, got), axis))


def body(samples, row_order, cluster_map, leaf_sketch, level_sketch):
    place = jnp.stack([lax.axis_index(a) for a in ("z", "y", "core", "x")]).astype(jnp.int32)
    rows = row_order.shape[1]
    rank = leaf_sketch.shape[1]
    row_norm = float(lax.axis_size("x") * samples.shape[0])
    first, second, send_a, send_b, keep_a, keep_b = prepare(
        samples, row_order, cluster_map, leaf_sketch, place
    )

    def to_cluster(packed):
        packed = packed.reshape(-1, 2 * rows, rank)
        return lax.all_to_all(packed, ("z", "y"), split_axis=0, concat_axis=0, tiled=True)

    got_a = swap(send_a, "core", 1)
    send_b, got_a = lax.optimization_barrier((send_b, got_a))
    got_b = swap(send_b, "core", 1)
    second = swap(second, "core", 1)
    keep_a, got_a = (v.reshape(8, 2, 8, -1, v.shape[-1]) for v in (keep_a, got_a))
    keep_b, got_b = (v.reshape(8, 2, 8, -1, v.shape[-1]) for v in (keep_b, got_b))
    term_a = lambda i, n: keep_a[i : i + n] + got_a[i : i + n]
    term_b = lambda i, n: keep_b[i : i + n] + got_b[i : i + n]
    sends_a, first = lax.optimization_barrier((ring_sends(term_a), first))
    sends_b = ring_sends(term_b)
    one_a = both_ways(sends_a, "x")
    one_b = both_ways(sends_b, "y")
    one_a = after(one_a, sends_b)
    two_a = both_ways(ring_lasts(term_a, one_a), "x")
    two_b = both_ways(ring_lasts(term_b, one_b), "y")
    low_a, high_a = ring_sum(term_a, one_a, two_a)
    low_b, high_b = ring_sum(term_b, one_b, two_b)
    first = to_cluster(first)
    part_a = jnp.concatenate([low_a, high_a], axis=0).reshape(8, 4, -1, low_a.shape[-1])
    part_b = jnp.concatenate([low_b, high_b], axis=0).reshape(8, 4, -1, low_b.shape[-1])
    low_a, high_a = scatter_ring(lambda i, n: part_a[i : i + n], "y")
    low_b, high_b = scatter_ring(lambda i, n: part_b[i : i + n], "x")
    part_a = jnp.concatenate([low_a, high_a], axis=0)
    part_b = jnp.concatenate([low_b, high_b], axis=0)
    total = jnp.concatenate([part_a, part_b], axis=1)
    total = total.reshape(4, 2, *total.shape[1:])
    total = total[0] + swap(total[1], "z", 2) + swap(total[2], "z", 1) + swap(total[3], "z", 3)
    second, total, first = lax.optimization_barrier((second, total, first))
    total = total[0] + swap(total[1], "z", 4)
    second = to_cluster(second)
    chunks = (total,) + tuple(swap(total, "x", mask) for mask in (1, 2, 3))
    parts, node = leaf_node(place, chunks, leaf_sketch, row_norm)
    halves = []
    for depth, (axis, bit) in enumerate((("core", 1), ("y", 1), ("y", 2))):
        other = swap(node, axis, bit)
        if depth == 1:
            basis, other = lax.optimization_barrier((bases(place, first, parts, 0), other))
        last = depth == LEVELS - 1
        half, node = merge(node, other, level_sketch[depth], halves if last else ())
        halves.append(half)
    basis = bases(place, second, parts, 1, basis).reshape(-1, rank)
    return (basis, halves[-1][None], node[None])


def solution(mesh):
    grid = Mesh(mesh.devices.reshape(8, 4, 2, 4), ("z", "y", "core", "x"))
    every = ("z", "y", "core", "x")
    leaf = ("z", "y", "core")
    in_specs = (P(every, None), P(every, None), P(every), P(), P())
    out_specs = (P(every, None), P(leaf, None, None, None), P(leaf, None, None))
    return jax.shard_map(body, mesh=grid, in_specs=in_specs, out_specs=out_specs, check_vma=False)
```
